32 devices in a mesh: grp: 4 (over z), row: 8 (over y, x, core).
Axes of the slice: x: 2, y: 2, z: 4, core: 2. Of those that a mesh axis runs over, the one named last changes fastest.
Arguments:
- design: bfloat16 [49152, 512], P(('grp', 'row')), may hold values from -0.29882812 to 0.29882812
- scales: bfloat16 [49152], P(('grp', 'row')), may hold values from 0.3984375 to 9.5
- buckets: int32 [49152], P(('grp', 'row')), may hold values from 0 to 1535
Outputs:
- sketch: float32 [6144, 512], P(('grp', 'row'))
- precond: float32 [512, 512], P('grp')
The draws below stay inside these ranges and needn't reach their ends.
All inputs are finite; a program needn't handle non-finite values.
Results may differ from the reference program's by a relative error of at most 0.0003.
Values sent between devices are 32-bit elements; how exact they have to be, the bound alone decides.
A program may use at most 64 MiB of HBM per device.

```python
import math
import jax
import jax.numpy as jnp
from jax import lax

D = 512
ROWS_DEV = 1536
ROWS = 49152
N_GRP = 4
N_ROW = 8


def place_ends(entries, own_key, least, largest):
    spot = [jax.random.randint(jax.random.fold_in(own_key, axis), (), 0, length) for axis, length in enumerate(entries.shape)]
    longest = entries.shape.index(max(entries.shape))
    next_to = spot[:longest] + [(spot[longest] + 1) % entries.shape[longest]] + spot[longest + 1:]
    return entries.at[tuple(spot)].set(least).at[tuple(next_to)].set(largest)


def block_levels(stream_key, extent, shards, least, top_value):
    def one(position, blocks):
        steps = jax.random.uniform(jax.random.fold_in(jax.random.fold_in(stream_key, 6), position), (blocks,), jnp.float32, least / len(shards), top_value / len(shards))
        return jnp.repeat(jnp.exp(steps), extent[position] // blocks).reshape((-1,) + (1,) * (len(extent) - position - 1))

    factor_of = one(*shards[0])
    for cut in shards[1:]:
        factor_of = factor_of * one(*cut)
    return factor_of


def scatter_about(rng, shape, deviation, most, split=(), kind=jnp.bfloat16):
    result = jax.random.normal(rng, shape, jnp.float32) * deviation
    if len(split) > 0:
        result = block_levels(rng, shape, split, -0.22, 0.18) * result
    return jnp.clip(result, min=-most, max=most).astype(kind)


def setup_inputs(seed: int = 0) -> dict:
    splits = jax.random.split(jax.random.key(seed), 4)
    return {
        "design": scatter_about(splits[0], (ROWS, D), 0.05, 0.29882812, ((0, 32),)),
        "scales": jnp.clip(jnp.exp(math.log(9.5) - 3.1714964 * jax.random.uniform(splits[1], (ROWS,), jnp.float32) ** block_levels(splits[1], (ROWS,), ((0, 32),), -0.2, 0.2)), 0.3984375, 9.5).astype(jnp.bfloat16),
        "buckets": place_ends(jax.random.randint(splits[2], (ROWS,), 0, ROWS_DEV), jax.random.fold_in(splits[2], 1), 0, ROWS_DEV - 1).astype(jnp.int32),
    }


def embed_group(pieces):
    rows_blk, weights, bucket_ids = pieces
    weighted = rows_blk.astype(jnp.float32) * weights.astype(jnp.float32)[:, None]
    return jax.ops.segment_sum(weighted, bucket_ids, num_segments=ROWS_DEV)

def reference(design, scales, buckets):
    per_group = ROWS_DEV * N_ROW
    grouped = (design.reshape(N_GRP, per_group, D), scales.reshape(N_GRP, per_group), buckets.reshape(N_GRP, per_group))
    sketch = lax.map(embed_group, grouped).reshape(N_GRP * ROWS_DEV, D)
    gram_matrix = jnp.dot(sketch.T.astype(jnp.float32), sketch.astype(jnp.float32), precision=lax.Precision.HIGHEST, preferred_element_type=jnp.float32)
    factor = jnp.linalg.cholesky(gram_matrix).T
    precond = factor / jnp.sqrt(jnp.float32(N_GRP * ROWS_DEV))
    return (sketch, precond)
```

```python
import functools
import math

import jax
import jax.numpy as jnp
from jax import lax
from jax.experimental import pallas as pl
from jax.experimental.pallas import tpu as pltpu
from jax.sharding import PartitionSpec as P

MESH = pl.DeviceIdType.MESH
F32 = jnp.float32
BF16 = jnp.bfloat16
LANES = 128
PANEL = 16


def split3(value):
    high = value.astype(BF16)
    rest = value - high.astype(F32)
    mid = rest.astype(BF16)
    low = (rest - mid.astype(F32)).astype(BF16)
    return high, mid, low


def panel_factor(panel, offset):
    size, width = panel.shape
    tiles = width // LANES
    sub = lax.broadcasted_iota(jnp.int32, (size, LANES), 0)
    cols = [
        jnp.broadcast_to(panel[:, offset + k : offset + k + 1], (size, LANES))
        for k in range(size)
    ]
    parts = [panel[:, t * LANES : (t + 1) * LANES] for t in range(tiles)]
    scale = jnp.zeros((size, LANES), F32)
    for j in range(size):
        inv = lax.rsqrt(cols[j][j : j + 1, :])
        mult = cols[j] * inv
        scale = jnp.where(sub == j, inv, scale)
        for k in range(j + 1, size):
            cols[k] = cols[k] - mult * (cols[k][j : j + 1, :] * inv)
        below = jnp.where(sub > j, mult, 0.0)
        parts = [part - below * (part[j : j + 1, :] * inv) for part in parts]
    return [part * scale for part in parts]


def factor_kernel(scale, grp_ref, gram_ref, out_ref, work):
    size = work.shape[0]
    half = size // 2
    quarter = size // 4
    for h in range(2):
        cs = slice(h * half, (h + 1) * half)
        work[0:quarter, cs] = gram_ref[h, 0:quarter, :]
    work[quarter : 2 * quarter, quarter:half] = gram_ref[0, quarter : 2 * quarter, quarter:half]
    work[quarter : 2 * quarter, half:size] = gram_ref[1, quarter : 2 * quarter, :]
    work[3 * quarter : size, 3 * quarter : size] = gram_ref[0, quarter : 2 * quarter, 0:quarter]
    work[half : half + quarter // 2, half:size] = gram_ref[0, half : half + quarter // 2, :]
    work[half + quarter // 2 : 3 * quarter, half:size] = gram_ref[1, half : half + quarter // 2, :]
    factor_in_place(work)
    write_rows(scale, grp_ref, out_ref, work)


def factor_whole_kernel(scale, grp_ref, gram_ref, out_ref, work):
    work[...] = gram_ref[...]
    factor_in_place(work)
    write_rows(scale, grp_ref, out_ref, work)


def factor_in_place(work):
    size = work.shape[0]
    for base in range(0, size, LANES):
        for start in range(0, LANES, PANEL):
            row = base + start
            rows = panel_factor(work[row : row + PANEL, base:size], start)
            for t, part in enumerate(rows):
                work[row : row + PANEL, base + t * LANES : base + (t + 1) * LANES] = part
            if start + PANEL == LANES:
                break
            splits = [split3(part) for part in rows]
            h, m, l = splits[0]
            lhs = jnp.concatenate([h, h, m, h, l, m], axis=0)
            for t, (h, m, l) in enumerate(splits):
                rhs = jnp.concatenate([h, m, h, l, h, m], axis=0)
                prod = lax.dot_general(
                    lhs, rhs, (((0,), (0,)), ((), ())), preferred_element_type=F32
                )
                cs = slice(base + t * LANES, base + (t + 1) * LANES)
                work[row + PANEL : base + LANES, cs] = (
                    work[row + PANEL : base + LANES, cs] - prod[start + PANEL :, :]
                )
        rest = base + LANES
        for left in range(rest, size, LANES):
            lhs = work[base:rest, left : left + LANES]
            work[left : left + LANES, left:size] = work[left : left + LANES, left:size] - lax.dot_general(
                lhs,
                work[base:rest, left:size],
                (((0,), (0,)), ((), ())),
                precision=lax.Precision.HIGHEST,
                preferred_element_type=F32,
            )


def write_rows(scale, grp_ref, out_ref, work):
    size = work.shape[0]
    count = out_ref.shape[0]
    first = pl.multiple_of(grp_ref[0] * count, count)
    rows = first + lax.broadcasted_iota(jnp.int32, (count, size), 0)
    cols = lax.broadcasted_iota(jnp.int32, (count, size), 1)
    value = work[pl.ds(first, count), :] * scale
    out_ref[...] = jnp.where(cols >= rows, value, 0.0)


def factor_call(kernel, gram, size, slab_rows, scale):
    grp = lax.axis_index("grp").astype(jnp.int32).reshape((1,))

    return pl.pallas_call(
        functools.partial(kernel, scale),
        out_shape=jax.ShapeDtypeStruct((slab_rows, size), F32),
        in_specs=[
            pl.BlockSpec(memory_space=pltpu.SMEM),
            pl.BlockSpec(memory_space=pltpu.VMEM),
        ],
        out_specs=pl.BlockSpec(memory_space=pltpu.VMEM),
        scratch_shapes=[pltpu.VMEM((size, size), F32)],
        compiler_params=pltpu.CompilerParams(vmem_limit_bytes=32 * 1024 * 1024),
        name="factor",
    )(grp, gram)


def self_gram(matrix):
    return lax.dot_general(
        matrix,
        matrix,
        (((0,), (0,)), ((), ())),
        precision=lax.Precision.HIGHEST,
        preferred_element_type=F32,
    )


def per_device_general(design, scales, buckets):
    row_count = design.shape[0]
    col_count = design.shape[1]
    row_parts = lax.axis_size("row")
    owned_rows = row_count // row_parts
    label_ids = lax.iota(jnp.int32, row_count)
    onehot_table = jnp.where(
        label_ids[:, None] == buckets[None, :], scales[None, :], jnp.zeros((), BF16)
    )
    partial_value = jnp.dot(onehot_table, design, preferred_element_type=F32).reshape(
        row_parts, owned_rows, col_count
    )
    arrived = lax.all_to_all(partial_value, "row", split_axis=0, concat_axis=0, tiled=True)
    sketch = jnp.sum(arrived, axis=0)
    whole_gram = lax.psum(self_gram(sketch), ("grp", "row"))
    grp_count = lax.axis_size("grp")
    scale = 1.0 / math.sqrt(row_count * grp_count)
    slab = factor_call(factor_whole_kernel, whole_gram, col_count, col_count // grp_count, scale)
    return (sketch, slab)


def embed_kernel(
    design_ref, scales_ref, buckets_ref, sketch_ref, gram_ref,
    give, took, acc, near, gsum, gcore, gown, gnear, gz, gall,
    give_s, give_r, near_s, near_r, gcore_s, gcore_r, gnear_s, gnear_r, gz_s, gz_r,
    gback_s, gback_r, gpair_s, gpair_r,
):
    z = lax.axis_index("grp")
    row = lax.axis_index("row")
    c = lax.rem(row, 2)
    x = lax.rem(row // 2, 2)
    y = row // 4
    core_id = (z, row + 1 - 2 * c)
    x_id = (z, row + 2 - 4 * x)
    y_id = (z, row + 4 - 8 * y)
    z_near_id = (z + 1 - 2 * lax.rem(z, 2), row)
    z_far_id = (z + 2 - 4 * (z // 2), row)
    peers = (core_id, x_id, y_id, z_near_id, z_far_id)

    barrier = pltpu.get_barrier_semaphore()
    for peer in peers:
        pl.semaphore_signal(barrier, inc=1, device_id=peer, device_id_type=MESH)
    pl.semaphore_wait(barrier, len(peers))

    pending = []

    def send(src, dst, send_sem, recv_sem, peer):
        copy = pltpu.make_async_remote_copy(
            src_ref=src, dst_ref=dst, send_sem=send_sem, recv_sem=recv_sem,
            device_id=peer, device_id_type=MESH,
        )
        copy.start()
        pending.append(copy)
        return copy

    rows_all = design_ref.shape[0]
    owned = sketch_ref.shape[0]
    half = design_ref.shape[1] // 2

    def part(slot, core):
        ty = y if slot < 2 else 1 - y
        tx = x if slot % 2 == 0 else 1 - x
        base = (ty * 4 + tx * 2 + core) * owned
        labels = base + lax.broadcasted_iota(jnp.int32, (owned, rows_all), 0)
        table = jnp.where(labels == buckets_ref[...], scales_ref[...], 0.0).astype(BF16)
        return jnp.dot(table, design_ref[...], preferred_element_type=F32)

    order = (3, 2, 1, 0)
    from_core = {}
    for s in order:
        value = part(s, 1 - c)
        give[s, 0] = value[:, :half]
        give[s, 1] = value[:, half:]
        from_core[s] = send(give.at[s], took.at[s], give_s.at[s], give_r.at[s], core_id)
    for s in order:
        value = part(s, c)
        acc[s, 0] = value[:, :half]
        acc[s, 1] = value[:, half:]

    first = (x_id, y_id)
    second = (y_id, x_id)
    passed = (2, 1)
    direct = (1, 2)

    def near_send(slot, h, step):
        peer = second[h] if step == 2 else first[h]
        return send(acc.at[slot, h], near.at[h, step], near_s.at[h, step], near_r.at[h, step], peer)

    steps = {}
    for s in order:
        from_core[s].wait_recv()
        for h in range(2):
            acc[s, h] = acc[s, h] + took[s, h]
            if s == 3:
                steps[h, 0] = near_send(3, h, 0)
            elif s == direct[h]:
                steps[h, 1] = near_send(s, h, 1)
    for h in range(2):
        steps[h, 0].wait_recv()
        acc[passed[h], h] = acc[passed[h], h] + near[h, 0]
        steps[h, 2] = near_send(passed[h], h, 2)
    for h in range(2):
        steps[h, 1].wait_recv()
        acc[0, h] = acc[0, h] + near[h, 1]
    for h in range(2):
        steps[h, 2].wait_recv()
        sketch_ref[:, h * half : (h + 1) * half] = acc[0, h] + near[h, 2]

    quarter = half // 2

    def block(i, j0, j1):
        return lax.dot_general(
            sketch_ref[:, i * quarter : (i + 1) * quarter],
            sketch_ref[:, j0 * quarter : j1 * quarter],
            (((0,), (0,)), ((), ())),
            precision=lax.Precision.HIGHEST,
            preferred_element_type=F32,
        )

    value = block(0, 0, 4)
    gsum[0, 0:quarter, :] = value[:, :half]
    gsum[1, 0:quarter, :] = value[:, half:]
    value = block(1, 1, 4)
    gsum[0, quarter:half, quarter:half] = value[:, :quarter]
    gsum[1, quarter:half, :] = value[:, quarter:]
    gsum[0, quarter:half, 0:quarter] = block(3, 3, 4)
    value = block(2, 2, 4)
    gsum[0, half:, :] = value[: quarter // 2, :]
    gsum[1, half:, :] = value[quarter // 2 :, :]

    packed = gsum.shape[1]
    core_rows = packed // 2
    piece = packed // 8
    theirs = pl.ds(pl.multiple_of((1 - c) * core_rows, 8), core_rows)
    ours = pl.ds(pl.multiple_of(c * core_rows, 8), core_rows)
    got = [
        send(gsum.at[h, theirs], gcore.at[h], gcore_s.at[h], gcore_r.at[h], core_id)
        for h in range(2)
    ]

    def chip(dy, dx):
        cy = 1 - y if dy else y
        cx = 1 - x if dx else x
        return pl.multiple_of((cy * 2 + cx) * piece, 8)

    def rows_of(dy, dx):
        return pl.ds(chip(dy, dx), piece)

    def gnear_send(dy, dx, h, step):
        peer = second[h] if step == 2 else first[h]
        return send(
            gown.at[h, rows_of(dy, dx)], gnear.at[h, step], gnear_s.at[h, step], gnear_r.at[h, step], peer
        )

    passed_at = ((1, 0), (0, 1))
    direct_at = ((0, 1), (1, 0))
    for h in range(2):
        got[h].wait_recv()
        gown[h] = gsum[h, ours] + gcore[h]
        steps[h, 0] = gnear_send(1, 1, h, 0)
        steps[h, 1] = gnear_send(*direct_at[h], h, 1)
    for h in range(2):
        steps[h, 0].wait_recv()
        rows = rows_of(*passed_at[h])
        gown[h, rows] = gown[h, rows] + gnear[h, 0]
        steps[h, 2] = gnear_send(*passed_at[h], h, 2)
    mine = rows_of(0, 0)
    for h in range(2):
        steps[h, 1].wait_recv()
        steps[h, 2].wait_recv()
        gown[h, mine] = (gown[h, mine] + gnear[h, 1]) + gnear[h, 2]

    keep = lax.rem(z, 2)
    at = pl.ds(pl.multiple_of(c * core_rows + chip(0, 0), 8), piece)
    copy = send(gown.at[1 - keep, mine], gz.at[0], gz_s.at[0], gz_r.at[0], z_near_id)
    copy.wait_recv()
    gz[2] = gown[keep, mine] + gz[0]
    copy = send(gz.at[2], gz.at[1], gz_s.at[1], gz_r.at[1], z_far_id)
    copy.wait_recv()
    gall[keep, at] = gz[2] + gz[1]
    copy = send(gall.at[keep, at], gall.at[keep, at], gz_s.at[2], gz_r.at[2], z_near_id)
    pltpu.make_async_remote_copy(
        src_ref=gall.at[1 - keep, at], dst_ref=gall.at[1 - keep, at],
        send_sem=gz_s.at[2], recv_sem=gz_r.at[2], device_id=z_near_id, device_id_type=MESH,
    ).wait_recv()

    def place(dy, dx, core):
        return pl.ds(pl.multiple_of(core * core_rows + chip(dy, dx), 8), piece)

    def back(dy, dx, h, step, peer):
        ref = gall.at[h, place(dy, dx, c)]
        return send(ref, ref, gback_s.at[h, step], gback_r.at[h, step], peer)

    def pair(dy, dx, h, step):
        ref = gall.at[h, place(dy, dx, c)]
        return send(ref, ref, gpair_s.at[h, step], gpair_r.at[h, step], core_id)

    def landed(dy, dx, core, h, sems, step):
        ref = gall.at[h, place(dy, dx, core)]
        pltpu.make_async_remote_copy(
            src_ref=ref, dst_ref=ref, send_sem=gback_s.at[h, step], recv_sem=sems.at[h, step],
            device_id=core_id, device_id_type=MESH,
        ).wait_recv()

    along = ((1, 0), (0, 1))
    across = ((0, 1), (1, 0))
    for h in range(2):
        back(0, 0, h, 0, second[h])
        back(0, 0, h, 1, first[h])
    for h in range(2):
        pair(0, 0, h, 0)
    for h in range(2):
        landed(*along[h], c, h, gback_r, 0)
        back(*along[h], h, 2, first[h])
        pair(*along[h], h, 1)
    for h in range(2):
        landed(*across[h], c, h, gback_r, 1)
        pair(*across[h], h, 2)
    for h in range(2):
        landed(1, 1, c, h, gback_r, 2)
        pair(1, 1, h, 3)
    for h in range(2):
        landed(0, 0, 1 - c, h, gpair_r, 0)
        landed(*along[h], 1 - c, h, gpair_r, 1)
        landed(*across[h], 1 - c, h, gpair_r, 2)
        landed(1, 1, 1 - c, h, gpair_r, 3)
    gram_ref[...] = gall[...]
    for copy in pending:
        copy.wait_send()


def per_device_fast(design, scales, buckets):
    row_count, col_count = design.shape
    owned = row_count // lax.axis_size("row")
    half = col_count // 2
    packed = col_count // 4 * 5 // 2
    piece = packed // 8
    dma = pltpu.SemaphoreType.DMA
    vmem = pl.BlockSpec(memory_space=pltpu.VMEM)
    sketch, gram = pl.pallas_call(
        embed_kernel,
        out_shape=(
            jax.ShapeDtypeStruct((owned, col_count), F32),
            jax.ShapeDtypeStruct((2, packed, half), F32),
        ),
        in_specs=[vmem] * 3,
        out_specs=(vmem, vmem),
        scratch_shapes=[
            pltpu.VMEM((4, 2, owned, half), F32),
            pltpu.VMEM((4, 2, owned, half), F32),
            pltpu.VMEM((4, 2, owned, half), F32),
            pltpu.VMEM((2, 3, owned, half), F32),
            pltpu.VMEM((2, packed, half), F32),
            pltpu.VMEM((2, packed // 2, half), F32),
            pltpu.VMEM((2, packed // 2, half), F32),
            pltpu.VMEM((2, 3, piece, half), F32),
            pltpu.VMEM((3, piece, half), F32),
            pltpu.VMEM((2, packed, half), F32),
            dma((4,)), dma((4,)),
            dma((2, 3)), dma((2, 3)),
            dma((2,)), dma((2,)),
            dma((2, 3)), dma((2, 3)),
            dma((3,)), dma((3,)),
            dma((2, 3)), dma((2, 3)),
            dma((2, 4)), dma((2, 4)),
        ],
        compiler_params=pltpu.CompilerParams(
            collective_id=0, has_side_effects=True, vmem_limit_bytes=40 * 1024 * 1024
        ),
        name="embed",
    )(design, scales.astype(F32).reshape(1, row_count), buckets.reshape(1, row_count))
    grp_count = lax.axis_size("grp")
    scale = 1.0 / math.sqrt(row_count * grp_count)
    slab = factor_call(factor_kernel, gram, col_count, col_count // grp_count, scale)
    return (sketch, slab)


def solution(mesh):
    in_specs = (P(("grp", "row"), None), P(("grp", "row")), P(("grp", "row")))
    out_specs = (P(("grp", "row"), None), P("grp", None))
    fast = mesh.shape["grp"] == 4 and mesh.shape["row"] == 8
    return jax.shard_map(
        per_device_fast if fast else per_device_general,
        mesh=mesh, in_specs=in_specs, out_specs=out_specs, check_vma=False,
    )
```

```python
import functools
import math

import jax
import jax.numpy as jnp
from jax import lax
from jax.experimental import pallas as pl
from jax.experimental.pallas import tpu as pltpu
from jax.sharding import PartitionSpec as P

MESH = pl.DeviceIdType.MESH
F32 = jnp.float32
BF16 = jnp.bfloat16
LANES = 128
PANEL = 16


def split3(value):
    high = value.astype(BF16)
    rest = value - high.astype(F32)
    mid = rest.astype(BF16)
    low = (rest - mid.astype(F32)).astype(BF16)
    return high, mid, low


def panel_factor(panel, offset):
    size, width = panel.shape
    tiles = width // LANES
    sub = lax.broadcasted_iota(jnp.int32, (size, LANES), 0)
    cols = [
        jnp.broadcast_to(panel[:, offset + k : offset + k + 1], (size, LANES))
        for k in range(size)
    ]
    parts = [panel[:, t * LANES : (t + 1) * LANES] for t in range(tiles)]
    scale = jnp.zeros((size, LANES), F32)
    for j in range(size):
        inv = lax.rsqrt(cols[j][j : j + 1, :])
        mult = cols[j] * inv
        scale = jnp.where(sub == j, inv, scale)
        for k in range(j + 1, size):
            cols[k] = cols[k] - mult * (cols[k][j : j + 1, :] * inv)
        below = jnp.where(sub > j, mult, 0.0)
        parts = [part - below * (part[j : j + 1, :] * inv) for part in parts]
    return [part * scale for part in parts]


def factor_kernel(scale, grp_ref, gram_ref, sketch_ref, out_ref, sketch_out, work, copy_sem):
    size = work.shape[0]
    copy = pltpu.make_async_copy(sketch_ref, sketch_out, copy_sem)
    copy.start()
    half = size // 2
    quarter = size // 4
    for h in range(2):
        cs = slice(h * half, (h + 1) * half)
        work[0:quarter, cs] = gram_ref[h, 0:quarter, :]
    work[quarter : 2 * quarter, quarter:half] = gram_ref[0, quarter : 2 * quarter, quarter:half]
    work[quarter : 2 * quarter, half:size] = gram_ref[1, quarter : 2 * quarter, :]
    work[3 * quarter : size, 3 * quarter : size] = gram_ref[0, quarter : 2 * quarter, 0:quarter]
    work[half : half + quarter // 2, half:size] = gram_ref[0, half : half + quarter // 2, :]
    work[half + quarter // 2 : 3 * quarter, half:size] = gram_ref[1, half : half + quarter // 2, :]
    factor_in_place(work)
    write_rows(scale, grp_ref, out_ref, work)
    copy.wait()


def factor_whole_kernel(scale, grp_ref, gram_ref, out_ref, work):
    work[...] = gram_ref[...]
    factor_in_place(work)
    write_rows(scale, grp_ref, out_ref, work)


def factor_in_place(work):
    size = work.shape[0]
    for base in range(0, size, LANES):
        for start in range(0, LANES, PANEL):
            row = base + start
            rows = panel_factor(work[row : row + PANEL, base:size], start)
            for t, part in enumerate(rows):
                work[row : row + PANEL, base + t * LANES : base + (t + 1) * LANES] = part
            if start + PANEL == LANES:
                break
            splits = [split3(part) for part in rows]
            h, m, l = splits[0]
            lhs = jnp.concatenate([h, h, m, h, l, m], axis=0)
            for t, (h, m, l) in enumerate(splits):
                rhs = jnp.concatenate([h, m, h, l, h, m], axis=0)
                prod = lax.dot_general(
                    lhs, rhs, (((0,), (0,)), ((), ())), preferred_element_type=F32
                )
                cs = slice(base + t * LANES, base + (t + 1) * LANES)
                work[row + PANEL : base + LANES, cs] = (
                    work[row + PANEL : base + LANES, cs] - prod[start + PANEL :, :]
                )
        rest = base + LANES
        for left in range(rest, size, LANES):
            lhs = work[base:rest, left : left + LANES]
            work[left : left + LANES, left:size] = work[left : left + LANES, left:size] - lax.dot_general(
                lhs,
                work[base:rest, left:size],
                (((0,), (0,)), ((), ())),
                precision=lax.Precision.HIGHEST,
                preferred_element_type=F32,
            )


def write_rows(scale, grp_ref, out_ref, work):
    size = work.shape[0]
    count = out_ref.shape[0]
    first = pl.multiple_of(grp_ref[0] * count, count)
    rows = first + lax.broadcasted_iota(jnp.int32, (count, size), 0)
    cols = lax.broadcasted_iota(jnp.int32, (count, size), 1)
    value = work[pl.ds(first, count), :] * scale
    out_ref[...] = jnp.where(cols >= rows, value, 0.0)


def factor_call(kernel, gram, size, slab_rows, scale, sketch=None):
    anywhere = pl.BlockSpec(memory_space=pl.ANY)
    vmem = pl.BlockSpec(memory_space=pltpu.VMEM)
    smem = pl.BlockSpec(memory_space=pltpu.SMEM)
    slab_shape = jax.ShapeDtypeStruct((slab_rows, size), F32)
    carried = sketch is not None
    grp = lax.axis_index("grp").astype(jnp.int32).reshape((1,))

    return pl.pallas_call(
        functools.partial(kernel, scale),
        out_shape=(slab_shape, jax.ShapeDtypeStruct(sketch.shape, F32)) if carried else slab_shape,
        in_specs=[smem, vmem, anywhere] if carried else [smem, vmem],
        out_specs=(vmem, anywhere) if carried else vmem,
        scratch_shapes=[pltpu.VMEM((size, size), F32)] + [pltpu.SemaphoreType.DMA] * carried,
        compiler_params=pltpu.CompilerParams(vmem_limit_bytes=32 * 1024 * 1024),
        name="factor",
    )(grp, gram, *([sketch] if carried else []))


def self_gram(matrix):
    return lax.dot_general(
        matrix,
        matrix,
        (((0,), (0,)), ((), ())),
        precision=lax.Precision.HIGHEST,
        preferred_element_type=F32,
    )


def per_device_general(design, scales, buckets):
    row_count = design.shape[0]
    col_count = design.shape[1]
    row_parts = lax.axis_size("row")
    owned_rows = row_count // row_parts
    label_ids = lax.iota(jnp.int32, row_count)
    onehot_table = jnp.where(
        label_ids[:, None] == buckets[None, :], scales[None, :], jnp.zeros((), BF16)
    )
    partial_value = jnp.dot(onehot_table, design, preferred_element_type=F32).reshape(
        row_parts, owned_rows, col_count
    )
    arrived = lax.all_to_all(partial_value, "row", split_axis=0, concat_axis=0, tiled=True)
    sketch = jnp.sum(arrived, axis=0)
    whole_gram = lax.psum(self_gram(sketch), ("grp", "row"))
    grp_count = lax.axis_size("grp")
    scale = 1.0 / math.sqrt(row_count * grp_count)
    slab = factor_call(factor_whole_kernel, whole_gram, col_count, col_count // grp_count, scale)
    return (sketch, slab)


def embed_kernel(
    design_hbm, scales_ref, buckets_ref, sketch_ref, gram_ref,
    design_ref, load_s, give, took, acc, near, gsum, gcore, gown, gnear, gz, gall,
    give_s, give_r, near_s, near_r, gcore_s, gcore_r, gnear_s, gnear_r, gz_s, gz_r,
    gback_s, gback_r, gpair_s, gpair_r,
):
    z = lax.axis_index("grp")
    row = lax.axis_index("row")
    c = lax.rem(row, 2)
    x = lax.rem(row // 2, 2)
    y = row // 4
    core_id = (z, row + 1 - 2 * c)
    x_id = (z, row + 2 - 4 * x)
    y_id = (z, row + 4 - 8 * y)
    z_near_id = (z + 1 - 2 * lax.rem(z, 2), row)
    z_far_id = (z + 2 - 4 * (z // 2), row)
    peers = (core_id, x_id, y_id, z_near_id, z_far_id)

    barrier = pltpu.get_barrier_semaphore()
    for peer in peers:
        pl.semaphore_signal(barrier, inc=1, device_id=peer, device_id_type=MESH)
    load = pltpu.make_async_copy(design_hbm, design_ref, load_s)
    load.start()

    pending = []

    def send(src, dst, send_sem, recv_sem, peer):
        copy = pltpu.make_async_remote_copy(
            src_ref=src, dst_ref=dst, send_sem=send_sem, recv_sem=recv_sem,
            device_id=peer, device_id_type=MESH,
        )
        copy.start()
        pending.append(copy)
        return copy

    rows_all = design_ref.shape[0]
    owned = sketch_ref.shape[0]
    half = design_ref.shape[1] // 2

    def part(slot):
        ty = y if slot < 2 else 1 - y
        tx = x if slot % 2 == 0 else 1 - x
        base = (ty * 4 + tx * 2) * owned
        ids = lax.broadcasted_iota(jnp.int32, (owned, LANES), 0) + base
        labels = jnp.concatenate([ids + (1 - c) * owned, ids + c * owned], axis=0)
        table = jnp.concatenate(
            [
                jnp.where(labels == buckets_ref[k : k + 1, :], scales_ref[k : k + 1, :], 0.0).astype(BF16)
                for k in range(rows_all // LANES)
            ],
            axis=1,
        )
        value = jnp.dot(table, design_ref[...], preferred_element_type=F32)
        for h in range(2):
            give[slot, h] = value[:owned, h * half : (h + 1) * half]
            acc[slot, h] = value[owned:, h * half : (h + 1) * half]

    first = (x_id, y_id)
    second = (y_id, x_id)
    passed = (2, 1)
    direct = (1, 2)

    def near_send(slot, h, step):
        peer = second[h] if step == 2 else first[h]
        return send(acc.at[slot, h], near.at[h, step], near_s.at[h, step], near_r.at[h, step], peer)

    steps = {}
    from_core = {}
    order = (3, 2, 1, 0)

    def give_core(slot):
        from_core[slot] = send(give.at[slot], took.at[slot], give_s.at[slot], give_r.at[slot], core_id)

    def take_core(slot):
        from_core[slot].wait_recv()
        for h in range(2):
            acc[slot, h] = acc[slot, h] + took[slot, h]
            if slot == 3:
                steps[h, 0] = near_send(slot, h, 0)
            elif slot == direct[h]:
                steps[h, 1] = near_send(slot, h, 1)

    load.wait()
    part(3)
    pl.semaphore_wait(barrier, len(peers))
    give_core(3)
    part(2)
    give_core(2)
    take_core(3)
    part(1)
    give_core(1)
    take_core(2)
    part(0)
    give_core(0)
    take_core(1)
    take_core(0)
    for h in range(2):
        steps[h, 0].wait_recv()
        acc[passed[h], h] = acc[passed[h], h] + near[h, 0]
        steps[h, 2] = near_send(passed[h], h, 2)
    for h in range(2):
        steps[h, 1].wait_recv()
        acc[0, h] = acc[0, h] + near[h, 1]
    for h in range(2):
        steps[h, 2].wait_recv()
        sketch_ref[:, h * half : (h + 1) * half] = acc[0, h] + near[h, 2]

    quarter = half // 2

    def block(i, j0, j1):
        return lax.dot_general(
            sketch_ref[:, i * quarter : (i + 1) * quarter],
            sketch_ref[:, j0 * quarter : j1 * quarter],
            (((0,), (0,)), ((), ())),
            precision=lax.Precision.HIGHEST,
            preferred_element_type=F32,
        )

    value = block(0, 0, 4)
    gsum[0, 0:quarter, :] = value[:, :half]
    gsum[1, 0:quarter, :] = value[:, half:]
    value = block(1, 1, 4)
    gsum[0, quarter:half, quarter:half] = value[:, :quarter]
    gsum[1, quarter:half, :] = value[:, quarter:]
    gsum[0, quarter:half, 0:quarter] = block(3, 3, 4)
    value = block(2, 2, 4)
    gsum[0, half:, :] = value[: quarter // 2, :]
    gsum[1, half:, :] = value[quarter // 2 :, :]

    packed = gsum.shape[1]
    core_rows = packed // 2
    piece = packed // 8
    theirs = pl.ds(pl.multiple_of((1 - c) * core_rows, 8), core_rows)
    ours = pl.ds(pl.multiple_of(c * core_rows, 8), core_rows)
    got = [
        send(gsum.at[h, theirs], gcore.at[h], gcore_s.at[h], gcore_r.at[h], core_id)
        for h in range(2)
    ]

    def chip(dy, dx):
        cy = 1 - y if dy else y
        cx = 1 - x if dx else x
        return pl.multiple_of((cy * 2 + cx) * piece, 8)

    def rows_of(dy, dx):
        return pl.ds(chip(dy, dx), piece)

    def gnear_send(dy, dx, h, step):
        peer = second[h] if step == 2 else first[h]
        return send(
            gown.at[h, rows_of(dy, dx)], gnear.at[h, step], gnear_s.at[h, step], gnear_r.at[h, step], peer
        )

    passed_at = ((1, 0), (0, 1))
    direct_at = ((0, 1), (1, 0))
    for h in range(2):
        got[h].wait_recv()
        gown[h] = gsum[h, ours] + gcore[h]
        steps[h, 0] = gnear_send(1, 1, h, 0)
        steps[h, 1] = gnear_send(*direct_at[h], h, 1)
    for h in range(2):
        steps[h, 0].wait_recv()
        rows = rows_of(*passed_at[h])
        gown[h, rows] = gown[h, rows] + gnear[h, 0]
        steps[h, 2] = gnear_send(*passed_at[h], h, 2)
    mine = rows_of(0, 0)
    for h in range(2):
        steps[h, 1].wait_recv()
        steps[h, 2].wait_recv()
        gown[h, mine] = (gown[h, mine] + gnear[h, 1]) + gnear[h, 2]

    keep = lax.rem(z, 2)
    at = pl.ds(pl.multiple_of(c * core_rows + chip(0, 0), 8), piece)
    copy = send(gown.at[1 - keep, mine], gz.at[0], gz_s.at[0], gz_r.at[0], z_near_id)
    copy.wait_recv()
    gz[2] = gown[keep, mine] + gz[0]
    copy = send(gz.at[2], gz.at[1], gz_s.at[1], gz_r.at[1], z_far_id)
    copy.wait_recv()
    gall[keep, at] = gz[2] + gz[1]
    copy = send(gall.at[keep, at], gall.at[keep, at], gz_s.at[2], gz_r.at[2], z_near_id)
    pltpu.make_async_remote_copy(
        src_ref=gall.at[1 - keep, at], dst_ref=gall.at[1 - keep, at],
        send_sem=gz_s.at[2], recv_sem=gz_r.at[2], device_id=z_near_id, device_id_type=MESH,
    ).wait_recv()

    def place(dy, dx, core):
        return pl.ds(pl.multiple_of(core * core_rows + chip(dy, dx), 8), piece)

    def back(dy, dx, h, step, peer):
        ref = gall.at[h, place(dy, dx, c)]
        return send(ref, ref, gback_s.at[h, step], gback_r.at[h, step], peer)

    def pair(dy, dx, h, step):
        ref = gall.at[h, place(dy, dx, c)]
        return send(ref, ref, gpair_s.at[h, step], gpair_r.at[h, step], core_id)

    def landed(dy, dx, core, h, sems, step):
        ref = gall.at[h, place(dy, dx, core)]
        pltpu.make_async_remote_copy(
            src_ref=ref, dst_ref=ref, send_sem=gback_s.at[h, step], recv_sem=sems.at[h, step],
            device_id=core_id, device_id_type=MESH,
        ).wait_recv()

    along = ((1, 0), (0, 1))
    across = ((0, 1), (1, 0))
    for h in range(2):
        back(0, 0, h, 0, second[h])
        back(0, 0, h, 1, first[h])
    for h in range(2):
        pair(0, 0, h, 0)
    for h in range(2):
        landed(*along[h], c, h, gback_r, 0)
        back(*along[h], h, 2, first[h])
        pair(*along[h], h, 1)
    for h in range(2):
        landed(*across[h], c, h, gback_r, 1)
        pair(*across[h], h, 2)
    for h in range(2):
        landed(1, 1, c, h, gback_r, 2)
        pair(1, 1, h, 3)
    for h in range(2):
        landed(0, 0, 1 - c, h, gpair_r, 0)
        landed(*along[h], 1 - c, h, gpair_r, 1)
        landed(*across[h], 1 - c, h, gpair_r, 2)
        landed(1, 1, 1 - c, h, gpair_r, 3)
    gram_ref[...] = gall[...]
    for copy in pending:
        copy.wait_send()


def per_device_fast(design, scales, buckets):
    row_count, col_count = design.shape
    owned = row_count // lax.axis_size("row")
    half = col_count // 2
    packed = col_count // 4 * 5 // 2
    piece = packed // 8
    dma = pltpu.SemaphoreType.DMA
    vmem = pl.BlockSpec(memory_space=pltpu.VMEM)
    sketch, gram = pl.pallas_call(
        embed_kernel,
        out_shape=(
            jax.ShapeDtypeStruct((owned, col_count), F32),
            jax.ShapeDtypeStruct((2, packed, half), F32),
        ),
        in_specs=[pl.BlockSpec(memory_space=pl.ANY), vmem, vmem],
        out_specs=(vmem, vmem),
        scratch_shapes=[
            pltpu.VMEM((row_count, col_count), BF16),
            pltpu.SemaphoreType.DMA,
            pltpu.VMEM((4, 2, owned, half), F32),
            pltpu.VMEM((4, 2, owned, half), F32),
            pltpu.VMEM((4, 2, owned, half), F32),
            pltpu.VMEM((2, 3, owned, half), F32),
            pltpu.VMEM((2, packed, half), F32),
            pltpu.VMEM((2, packed // 2, half), F32),
            pltpu.VMEM((2, packed // 2, half), F32),
            pltpu.VMEM((2, 3, piece, half), F32),
            pltpu.VMEM((3, piece, half), F32),
            pltpu.VMEM((2, packed, half), F32),
            dma((4,)), dma((4,)),
            dma((2, 3)), dma((2, 3)),
            dma((2,)), dma((2,)),
            dma((2, 3)), dma((2, 3)),
            dma((3,)), dma((3,)),
            dma((2, 3)), dma((2, 3)),
            dma((2, 4)), dma((2, 4)),
        ],
        compiler_params=pltpu.CompilerParams(
            collective_id=0, has_side_effects=True, vmem_limit_bytes=60 * 1024 * 1024
        ),
        name="embed",
    )(design, scales.astype(F32).reshape(-1, LANES), buckets.reshape(-1, LANES))
    grp_count = lax.axis_size("grp")
    scale = 1.0 / math.sqrt(row_count * grp_count)
    slab, sketch = factor_call(factor_kernel, gram, col_count, col_count // grp_count, scale, sketch)
    return (sketch, slab)


def solution(mesh):
    in_specs = (P(("grp", "row"), None), P(("grp", "row")), P(("grp", "row")))
    out_specs = (P(("grp", "row"), None), P("grp", None))
    fast = mesh.shape["grp"] == 4 and mesh.shape["row"] == 8
    return jax.shard_map(
        per_device_fast if fast else per_device_general,
        mesh=mesh, in_specs=in_specs, out_specs=out_specs, check_vma=False,
    )
```

```python
import functools
import math

import jax
import jax.numpy as jnp
from jax import lax
from jax.experimental import pallas as pl
from jax.experimental.pallas import tpu as pltpu
from jax.sharding import PartitionSpec as P

MESH = pl.DeviceIdType.MESH
F32 = jnp.float32
BF16 = jnp.bfloat16
LANES = 128
PANEL = 16


def split3(value):
    high = value.astype(BF16)
    rest = value - high.astype(F32)
    mid = rest.astype(BF16)
    low = (rest - mid.astype(F32)).astype(BF16)
    return high, mid, low


def panel_factor(panel, offset):
    size, width = panel.shape
    tiles = width // LANES
    sub = lax.broadcasted_iota(jnp.int32, (size, LANES), 0)
    cols = [
        jnp.broadcast_to(panel[:, offset + k : offset + k + 1], (size, LANES))
        for k in range(size)
    ]
    parts = [panel[:, t * LANES : (t + 1) * LANES] for t in range(tiles)]
    scale = jnp.zeros((size, LANES), F32)
    for j in range(size):
        inv = lax.rsqrt(cols[j][j : j + 1, :])
        mult = cols[j] * inv
        scale = jnp.where(sub == j, inv, scale)
        for k in range(j + 1, size):
            cols[k] = cols[k] - mult * (cols[k][j : j + 1, :] * inv)
        below = jnp.where(sub > j, mult, 0.0)
        parts = [part - below * (part[j : j + 1, :] * inv) for part in parts]
    return [part * scale for part in parts]


def factor_block(work, base, stop, hook=None):
    for start in range(0, LANES, PANEL):
        row = base + start
        rows = panel_factor(work[row : row + PANEL, base:stop], start)
        for t, part in enumerate(rows):
            work[row : row + PANEL, base + t * LANES : base + (t + 1) * LANES] = part
        if hook is not None:
            hook()
        if start + PANEL == LANES:
            break
        splits = [split3(part) for part in rows]
        h, m, l = splits[0]
        lhs = jnp.concatenate([h, h, m, h, l, m], axis=0)
        for t, (h, m, l) in enumerate(splits):
            rhs = jnp.concatenate([h, m, h, l, h, m], axis=0)
            prod = lax.dot_general(lhs, rhs, (((0,), (0,)), ((), ())), preferred_element_type=F32)
            cs = slice(base + t * LANES, base + (t + 1) * LANES)
            work[row + PANEL : base + LANES, cs] = (
                work[row + PANEL : base + LANES, cs] - prod[start + PANEL :, :]
            )


def tdot(left, right):
    return lax.dot_general(
        left, right, (((0,), (0,)), ((), ())),
        precision=lax.Precision.HIGHEST, preferred_element_type=F32,
    )


def trail(work, base, last, stop):
    for left in range(base + LANES, last, LANES):
        work[left : left + LANES, left:stop] = work[left : left + LANES, left:stop] - tdot(
            work[base : base + LANES, left : left + LANES], work[base : base + LANES, left:stop]
        )


def write_rows(grp, scale, out_ref, work):
    size = work.shape[0]
    count = out_ref.shape[0]
    first = pl.multiple_of(grp * count, count)
    rows = first + lax.broadcasted_iota(jnp.int32, (count, size), 0)
    cols = lax.broadcasted_iota(jnp.int32, (count, size), 1)
    value = work[pl.ds(first, count), :] * scale
    out_ref[...] = jnp.where(cols >= rows, value, 0.0)


def factor_kernel(scale, gram_ref, out_ref, work):
    size = work.shape[0]
    work[...] = gram_ref[...]
    for base in range(0, size, LANES):
        factor_block(work, base, size)
        trail(work, base, size, size)
    write_rows(lax.axis_index("grp"), scale, out_ref, work)


def factor_call(gram, slab_rows, scale):
    size = gram.shape[0]
    vmem = pl.BlockSpec(memory_space=pltpu.VMEM)
    return pl.pallas_call(
        functools.partial(factor_kernel, scale),
        out_shape=jax.ShapeDtypeStruct((slab_rows, size), F32),
        in_specs=[vmem],
        out_specs=vmem,
        scratch_shapes=[pltpu.VMEM((size, size), F32)],
        compiler_params=pltpu.CompilerParams(vmem_limit_bytes=32 * 1024 * 1024),
        name="factor",
    )(gram)


def self_gram(matrix):
    return lax.dot_general(
        matrix,
        matrix,
        (((0,), (0,)), ((), ())),
        precision=lax.Precision.HIGHEST,
        preferred_element_type=F32,
    )


def per_device_general(design, scales, buckets):
    row_count = design.shape[0]
    col_count = design.shape[1]
    row_parts = lax.axis_size("row")
    owned_rows = row_count // row_parts
    label_ids = lax.iota(jnp.int32, row_count)
    onehot_table = jnp.where(
        label_ids[:, None] == buckets[None, :], scales[None, :], jnp.zeros((), BF16)
    )
    partial_value = jnp.dot(onehot_table, design, preferred_element_type=F32).reshape(
        row_parts, owned_rows, col_count
    )
    arrived = lax.all_to_all(partial_value, "row", split_axis=0, concat_axis=0, tiled=True)
    sketch = jnp.sum(arrived, axis=0)
    whole_gram = lax.psum(self_gram(sketch), ("grp", "row"))
    grp_count = lax.axis_size("grp")
    scale = 1.0 / math.sqrt(row_count * grp_count)
    slab = factor_call(whole_gram, col_count // grp_count, scale)
    return (sketch, slab)


def embed_kernel(
    scale, design_hbm, scales_in, buckets_ref, sketch_out, out_ref,
    design_ref, load_s, sketch_ref, store_s, scales_ref, work,
    give, took, acc, near, give_s, give_r, near_s, near_r, *chunk_refs,
):
    z = lax.axis_index("grp")
    row = lax.axis_index("row")
    c = lax.rem(row, 2)
    x = lax.rem(row // 2, 2)
    y = row // 4
    core_id = (z, row + 1 - 2 * c)
    x_id = (z, row + 2 - 4 * x)
    y_id = (z, row + 4 - 8 * y)
    z_near_id = (z + 1 - 2 * lax.rem(z, 2), row)
    z_far_id = (z + 2 - 4 * (z // 2), row)
    peers = (core_id, x_id, y_id, z_near_id, z_far_id)

    barrier = pltpu.get_barrier_semaphore()
    for peer in peers:
        pl.semaphore_signal(barrier, inc=1, device_id=peer, device_id_type=MESH)
    load = pltpu.make_async_copy(design_hbm, design_ref, load_s)
    load.start()

    pending = []

    def send(src, dst, send_sem, recv_sem, peer):
        copy = pltpu.make_async_remote_copy(
            src_ref=src, dst_ref=dst, send_sem=send_sem, recv_sem=recv_sem,
            device_id=peer, device_id_type=MESH,
        )
        copy.start()
        pending.append(copy)
        return copy

    scales_ref[...] = scales_in[...].astype(F32)
    work[...] = jnp.zeros_like(work)
    rows_all = design_ref.shape[0]
    owned = sketch_ref.shape[0]
    half = design_ref.shape[1] // 2

    def part(slot):
        ty = y if slot < 2 else 1 - y
        tx = x if slot % 2 == 0 else 1 - x
        base = (ty * 4 + tx * 2) * owned
        ids = lax.broadcasted_iota(jnp.int32, (owned, LANES), 0) + base
        labels = jnp.concatenate([ids + (1 - c) * owned, ids + c * owned], axis=0)
        table = jnp.concatenate(
            [
                jnp.where(labels == buckets_ref[k : k + 1, :], scales_ref[k : k + 1, :], 0.0).astype(BF16)
                for k in range(rows_all // LANES)
            ],
            axis=1,
        )
        value = jnp.dot(table, design_ref[...], preferred_element_type=F32)
        for h in range(2):
            give[slot, h] = value[:owned, h * half : (h + 1) * half]
            acc[slot, h] = value[owned:, h * half : (h + 1) * half]

    first = (x_id, y_id)
    second = (y_id, x_id)
    passed = (2, 1)
    direct = (1, 2)

    def near_send(slot, h, step):
        peer = second[h] if step == 2 else first[h]
        return send(acc.at[slot, h], near.at[h, step], near_s.at[h, step], near_r.at[h, step], peer)

    steps = {}
    from_core = {}
    order = (3, 2, 1, 0)

    def give_core(slot):
        from_core[slot] = send(give.at[slot], took.at[slot], give_s.at[slot], give_r.at[slot], core_id)

    def take_core(slot):
        from_core[slot].wait_recv()
        for h in range(2):
            acc[slot, h] = acc[slot, h] + took[slot, h]
            if slot == 3:
                steps[h, 0] = near_send(slot, h, 0)
            elif slot == direct[h]:
                steps[h, 1] = near_send(slot, h, 1)

    load.wait()
    part(3)
    pl.semaphore_wait(barrier, len(peers))
    give_core(3)
    part(2)
    give_core(2)
    take_core(3)
    part(1)
    give_core(1)
    take_core(2)
    part(0)
    give_core(0)
    take_core(1)
    take_core(0)
    for h in range(2):
        steps[h, 0].wait_recv()
        acc[passed[h], h] = acc[passed[h], h] + near[h, 0]
        steps[h, 2] = near_send(passed[h], h, 2)
    for h in range(2):
        steps[h, 1].wait_recv()
        acc[0, h] = acc[0, h] + near[h, 1]
    for h in range(2):
        steps[h, 2].wait_recv()
        sketch_ref[:, h * half : (h + 1) * half] = acc[0, h] + near[h, 2]

    store = pltpu.make_async_copy(sketch_ref, sketch_out, store_s)
    store.start()

    def chip(dy, dx, piece):
        cy = 1 - y if dy else y
        cx = 1 - x if dx else x
        return pl.multiple_of((cy * 2 + cx) * piece, 8)

    passed_at = ((1, 0), (0, 1))
    direct_at = ((0, 1), (1, 0))

    def all_reduce(refs):
        (gsum, gcore, gown, gnear, gz, gall, gcore_s, gcore_r, gnear_s, gnear_r,
         gz_s, gz_r, gback_s, gback_r, gpair_s, gpair_r) = refs
        packed = gsum.shape[1]
        core_rows = packed // 2
        piece = packed // 8
        theirs = pl.ds(pl.multiple_of((1 - c) * core_rows, 8), core_rows)
        ours = pl.ds(pl.multiple_of(c * core_rows, 8), core_rows)
        got = [
            send(gsum.at[h, theirs], gcore.at[h], gcore_s.at[h], gcore_r.at[h], core_id)
            for h in range(2)
        ]
        yield

        def rows_of(dy, dx):
            return pl.ds(chip(dy, dx, piece), piece)

        def gnear_send(dy, dx, h, step):
            peer = second[h] if step == 2 else first[h]
            return send(
                gown.at[h, rows_of(dy, dx)], gnear.at[h, step],
                gnear_s.at[h, step], gnear_r.at[h, step], peer,
            )

        hops = {}
        for h in range(2):
            got[h].wait_recv()
            gown[h] = gsum[h, ours] + gcore[h]
            hops[h, 0] = gnear_send(1, 1, h, 0)
            hops[h, 1] = gnear_send(*direct_at[h], h, 1)
        yield
        for h in range(2):
            hops[h, 0].wait_recv()
            rows = rows_of(*passed_at[h])
            gown[h, rows] = gown[h, rows] + gnear[h, 0]
            hops[h, 2] = gnear_send(*passed_at[h], h, 2)
        yield
        mine = rows_of(0, 0)
        for h in range(2):
            hops[h, 1].wait_recv()
            hops[h, 2].wait_recv()
            gown[h, mine] = (gown[h, mine] + gnear[h, 1]) + gnear[h, 2]

        keep = lax.rem(z, 2)
        at = pl.ds(pl.multiple_of(c * core_rows + chip(0, 0, piece), 8), piece)
        copy = send(gown.at[1 - keep, mine], gz.at[0], gz_s.at[0], gz_r.at[0], z_near_id)
        yield
        copy.wait_recv()
        gz[2] = gown[keep, mine] + gz[0]
        copy = send(gz.at[2], gz.at[1], gz_s.at[1], gz_r.at[1], z_far_id)
        yield
        copy.wait_recv()
        gall[keep, at] = gz[2] + gz[1]
        send(gall.at[keep, at], gall.at[keep, at], gz_s.at[2], gz_r.at[2], z_near_id)
        yield
        pltpu.make_async_remote_copy(
            src_ref=gall.at[1 - keep, at], dst_ref=gall.at[1 - keep, at],
            send_sem=gz_s.at[2], recv_sem=gz_r.at[2], device_id=z_near_id, device_id_type=MESH,
        ).wait_recv()

        def place(dy, dx, core):
            return pl.ds(pl.multiple_of(core * core_rows + chip(dy, dx, piece), 8), piece)

        def back(dy, dx, h, step, peer):
            ref = gall.at[h, place(dy, dx, c)]
            return send(ref, ref, gback_s.at[h, step], gback_r.at[h, step], peer)

        def pair(dy, dx, h, step):
            ref = gall.at[h, place(dy, dx, c)]
            return send(ref, ref, gpair_s.at[h, step], gpair_r.at[h, step], core_id)

        def landed(dy, dx, core, h, sems, step):
            ref = gall.at[h, place(dy, dx, core)]
            pltpu.make_async_remote_copy(
                src_ref=ref, dst_ref=ref, send_sem=gback_s.at[h, 0], recv_sem=sems.at[h, step],
                device_id=core_id, device_id_type=MESH,
            ).wait_recv()

        for h in range(2):
            back(0, 0, h, 0, second[h])
            back(0, 0, h, 1, first[h])
        for h in range(2):
            pair(0, 0, h, 0)
        yield
        for h in range(2):
            landed(*passed_at[h], c, h, gback_r, 0)
            back(*passed_at[h], h, 2, first[h])
            pair(*passed_at[h], h, 1)
        yield
        for h in range(2):
            landed(*direct_at[h], c, h, gback_r, 1)
            pair(*direct_at[h], h, 2)
        for h in range(2):
            landed(1, 1, c, h, gback_r, 2)
            pair(1, 1, h, 3)
        yield
        for h in range(2):
            landed(0, 0, 1 - c, h, gpair_r, 0)
            landed(*passed_at[h], 1 - c, h, gpair_r, 1)
            landed(*direct_at[h], 1 - c, h, gpair_r, 2)
            landed(1, 1, 1 - c, h, gpair_r, 3)

    q = half // 2
    chunk_a, chunk_b = chunk_refs[:16], chunk_refs[16:]

    def cut(i, j=None):
        return sketch_ref[:, i * q : (i + 1 if j is None else j) * q]

    gsum = chunk_a[0]
    value = tdot(cut(0), cut(0, 2))
    gsum[0, 0:q] = value[:, :q]
    gsum[1, 0:q] = value[:, q:]
    value = tdot(cut(1), cut(1))
    gsum[0, q:] = value[: q // 2]
    gsum[1, q:] = value[q // 2 :]
    steps_a = all_reduce(chunk_a)
    next(steps_a)
    gsum = chunk_b[0]
    for i in range(3):
        value = tdot(cut(i), cut(2, 4))
        gsum[0, i * q : (i + 1) * q] = value[:, :q]
        gsum[1, i * q : (i + 1) * q] = value[:, q:]
    value = tdot(cut(3), cut(3))
    gsum[0, 3 * q :] = value[: q // 2]
    gsum[1, 3 * q :] = value[q // 2 :]
    steps_b = all_reduce(chunk_b)

    def run(steps, count=1):
        for _ in range(count):
            next(steps, None)

    run(steps_b)
    for _ in range(4):
        run(steps_a, 2)
        run(steps_b)
    run(steps_a, 2)

    gall = chunk_a[5]
    work[0:q, 0:q] = gall[0, 0:q]
    work[0:q, q:half] = gall[1, 0:q]
    work[q : q + q // 2, q:half] = gall[0, q:]
    work[q + q // 2 : half, q:half] = gall[1, q:]
    eye = (
        lax.broadcasted_iota(jnp.int32, (q, q), 0) == lax.broadcasted_iota(jnp.int32, (q, q), 1)
    ).astype(F32)
    work[0:q, half : half + q] = eye
    work[q:half, half + q :] = eye
    calls = []

    def hook():
        calls.append(0)
        if len(calls) % 2 == 0:
            run(steps_b)

    factor_block(work, 0, half + q, hook)
    trail(work, 0, half, half + q)
    factor_block(work, q, 2 * half, hook)
    for _ in steps_b:
        pass

    gall = chunk_b[5]
    right = jnp.concatenate([gall[0, :half], gall[1, :half]], axis=1)
    solved = lax.dot_general(
        work[0:half, half:], right, (((1,), (0,)), ((), ())),
        precision=lax.Precision.HIGHEST, preferred_element_type=F32,
    )
    work[0:half, half:] = solved
    prod = tdot(solved, solved)
    work[half : half + q, half : half + q] = gall[0, half : half + q] - prod[:q, :q]
    work[half : half + q, half + q :] = gall[1, half : half + q] - prod[:q, q:]
    work[half + q : half + q + q // 2, half + q :] = gall[0, 3 * q :] - prod[q : q + q // 2, q:]
    work[half + q + q // 2 :, half + q :] = gall[1, 3 * q :] - prod[q + q // 2 :, q:]
    factor_block(work, half, 2 * half)
    trail(work, half, 2 * half, 2 * half)
    factor_block(work, half + q, 2 * half)
    write_rows(z, scale, out_ref, work)
    store.wait()
    for copy in pending:
        copy.wait_send()


def chunk_scratch(packed, lanes):
    piece = packed // 8
    dma = pltpu.SemaphoreType.DMA
    return [
        pltpu.VMEM((2, packed, lanes), F32),
        pltpu.VMEM((2, packed // 2, lanes), F32),
        pltpu.VMEM((2, packed // 2, lanes), F32),
        pltpu.VMEM((2, 3, piece, lanes), F32),
        pltpu.VMEM((3, piece, lanes), F32),
        pltpu.VMEM((2, packed, lanes), F32),
        dma((2,)), dma((2,)),
        dma((2, 3)), dma((2, 3)),
        dma((3,)), dma((3,)),
        dma((2, 3)), dma((2, 3)),
        dma((2, 4)), dma((2, 4)),
    ]


def per_device_fast(design, scales, buckets):
    row_count, col_count = design.shape
    owned = row_count // lax.axis_size("row")
    half = col_count // 2
    quarter = half // 2
    grp_count = lax.axis_size("grp")
    dma = pltpu.SemaphoreType.DMA
    vmem = pl.BlockSpec(memory_space=pltpu.VMEM)
    return pl.pallas_call(
        functools.partial(embed_kernel, 1.0 / math.sqrt(row_count * grp_count)),
        out_shape=(
            jax.ShapeDtypeStruct((owned, col_count), F32),
            jax.ShapeDtypeStruct((col_count // grp_count, col_count), F32),
        ),
        in_specs=[pl.BlockSpec(memory_space=pl.ANY), vmem, vmem],
        out_specs=(pl.BlockSpec(memory_space=pl.ANY), vmem),
        scratch_shapes=[
            pltpu.VMEM((row_count, col_count), BF16),
            dma,
            pltpu.VMEM((owned, col_count), F32),
            dma,
            pltpu.VMEM((row_count // LANES, LANES), F32),
            pltpu.VMEM((col_count, col_count), F32),
            pltpu.VMEM((4, 2, owned, half), F32),
            pltpu.VMEM((4, 2, owned, half), F32),
            pltpu.VMEM((4, 2, owned, half), F32),
            pltpu.VMEM((2, 3, owned, half), F32),
            dma((4,)), dma((4,)),
            dma((2, 3)), dma((2, 3)),
        ]
        + chunk_scratch(quarter * 3 // 2, quarter)
        + chunk_scratch(quarter * 7 // 2, quarter),
        compiler_params=pltpu.CompilerParams(
            collective_id=0, has_side_effects=True, vmem_limit_bytes=60 * 1024 * 1024
        ),
        name="embed",
    )(design, scales.reshape(-1, LANES), buckets.reshape(-1, LANES))


def solution(mesh):
    in_specs = (P(("grp", "row"), None), P(("grp", "row")), P(("grp", "row")))
    out_specs = (P(("grp", "row"), None), P("grp", None))
    fast = mesh.shape["grp"] == 4 and mesh.shape["row"] == 8
    return jax.shard_map(
        per_device_fast if fast else per_device_general,
        mesh=mesh, in_specs=in_specs, out_specs=out_specs, check_vma=False,
    )
```

```python
import functools
import math

import jax
import jax.numpy as jnp
from jax import lax
from jax.experimental import pallas as pl
from jax.experimental.pallas import tpu as pltpu
from jax.sharding import PartitionSpec as P

MESH = pl.DeviceIdType.MESH
F32 = jnp.float32
BF16 = jnp.bfloat16
LANES = 128
PANEL = 16


def split3(value):
    high = value.astype(BF16)
    rest = value - high.astype(F32)
    mid = rest.astype(BF16)
    low = (rest - mid.astype(F32)).astype(BF16)
    return high, mid, low


def panel_factor(panel, offset):
    size, width = panel.shape
    tiles = width // LANES
    sub = lax.broadcasted_iota(jnp.int32, (size, LANES), 0)
    cols = [
        jnp.broadcast_to(panel[:, offset + k : offset + k + 1], (size, LANES))
        for k in range(size)
    ]
    parts = [panel[:, t * LANES : (t + 1) * LANES] for t in range(tiles)]
    scale = jnp.zeros((size, LANES), F32)
    for j in range(size):
        inv = lax.rsqrt(cols[j][j : j + 1, :])
        mult = cols[j] * inv
        scale = jnp.where(sub == j, inv, scale)
        for k in range(j + 1, size):
            cols[k] = cols[k] - mult * (cols[k][j : j + 1, :] * inv)
        below = jnp.where(sub > j, mult, 0.0)
        parts = [part - below * (part[j : j + 1, :] * inv) for part in parts]
    return [part * scale for part in parts]


def factor_block(work, base, stop, hook=None):
    for start in range(0, LANES, PANEL):
        row = base + start
        rows = panel_factor(work[row : row + PANEL, base:stop], start)
        for t, part in enumerate(rows):
            work[row : row + PANEL, base + t * LANES : base + (t + 1) * LANES] = part
        if hook is not None:
            hook()
        if start + PANEL == LANES:
            break
        splits = [split3(part) for part in rows]
        h, m, l = splits[0]
        lhs = jnp.concatenate([h, h, m, h, l, m], axis=0)
        for t, (h, m, l) in enumerate(splits):
            rhs = jnp.concatenate([h, m, h, l, h, m], axis=0)
            prod = lax.dot_general(lhs, rhs, (((0,), (0,)), ((), ())), preferred_element_type=F32)
            cs = slice(base + t * LANES, base + (t + 1) * LANES)
            work[row + PANEL : base + LANES, cs] = (
                work[row + PANEL : base + LANES, cs] - prod[start + PANEL :, :]
            )


def tdot(left, right):
    return lax.dot_general(
        left, right, (((0,), (0,)), ((), ())),
        precision=lax.Precision.HIGHEST, preferred_element_type=F32,
    )


def trail(work, base, last, stop):
    for left in range(base + LANES, last, LANES):
        work[left : left + LANES, left:stop] = work[left : left + LANES, left:stop] - tdot(
            work[base : base + LANES, left : left + LANES], work[base : base + LANES, left:stop]
        )


def write_rows(grp, scale, out_ref, work):
    size = work.shape[0]
    count = out_ref.shape[0]
    first = pl.multiple_of(grp * count, count)
    rows = first + lax.broadcasted_iota(jnp.int32, (count, size), 0)
    cols = lax.broadcasted_iota(jnp.int32, (count, size), 1)
    value = work[pl.ds(first, count), :] * scale
    out_ref[...] = jnp.where(cols >= rows, value, 0.0)


def factor_kernel(scale, gram_ref, out_ref, work):
    size = work.shape[0]
    work[...] = gram_ref[...]
    for base in range(0, size, LANES):
        factor_block(work, base, size)
        trail(work, base, size, size)
    write_rows(lax.axis_index("grp"), scale, out_ref, work)


def factor_packed_kernel(scale, gram_ref, sketch_ref, out_ref, sketch_out, work, copy_sem):
    copy = pltpu.make_async_copy(sketch_ref, sketch_out, copy_sem)
    copy.start()
    size = work.shape[0]
    half = size // 2
    q = half // 2
    work[0:q] = gram_ref[0:q]
    work[q:half, q:] = gram_ref[q:half, q:]
    work[3 * q :, 3 * q :] = gram_ref[q:half, 0:q]
    work[half : half + q // 2, half:] = gram_ref[half:, 0:half]
    work[half + q // 2 : 3 * q, half:] = gram_ref[half:, half:]
    for base in range(0, size, LANES):
        factor_block(work, base, size)
        trail(work, base, size, size)
    write_rows(lax.axis_index("grp"), scale, out_ref, work)
    copy.wait()


def factor_call(gram, slab_rows, scale):
    size = gram.shape[0]
    vmem = pl.BlockSpec(memory_space=pltpu.VMEM)
    return pl.pallas_call(
        functools.partial(factor_kernel, scale),
        out_shape=jax.ShapeDtypeStruct((slab_rows, size), F32),
        in_specs=[vmem],
        out_specs=vmem,
        scratch_shapes=[pltpu.VMEM((size, size), F32)],
        compiler_params=pltpu.CompilerParams(vmem_limit_bytes=32 * 1024 * 1024),
        name="factor",
    )(gram)


def self_gram(matrix):
    return lax.dot_general(
        matrix,
        matrix,
        (((0,), (0,)), ((), ())),
        precision=lax.Precision.HIGHEST,
        preferred_element_type=F32,
    )


def per_device_general(design, scales, buckets):
    row_count = design.shape[0]
    col_count = design.shape[1]
    row_parts = lax.axis_size("row")
    owned_rows = row_count // row_parts
    label_ids = lax.iota(jnp.int32, row_count)
    onehot_table = jnp.where(
        label_ids[:, None] == buckets[None, :], scales[None, :], jnp.zeros((), BF16)
    )
    partial_value = jnp.dot(onehot_table, design, preferred_element_type=F32).reshape(
        row_parts, owned_rows, col_count
    )
    arrived = lax.all_to_all(partial_value, "row", split_axis=0, concat_axis=0, tiled=True)
    sketch = jnp.sum(arrived, axis=0)
    whole_gram = lax.psum(self_gram(sketch), ("grp", "row"))
    grp_count = lax.axis_size("grp")
    scale = 1.0 / math.sqrt(row_count * grp_count)
    slab = factor_call(whole_gram, col_count // grp_count, scale)
    return (sketch, slab)


def embed_kernel(
    design_ref, scales_in, buckets_ref, sketch_ref, gram_ref, scales_ref,
    give, took, acc, near, gsum, gcore, gown, gnear, gz, gquart, gall,
    give_s, give_r, near_s, near_r, gcore_s, gcore_r, gnear_s, gnear_r, gz_s, gz_r,
    gback_s, gback_r, gpair_s, gpair_r,
):
    z = lax.axis_index("grp")
    row = lax.axis_index("row")
    c = lax.rem(row, 2)
    x = lax.rem(row // 2, 2)
    y = row // 4
    core_id = (z, row + 1 - 2 * c)
    x_id = (z, row + 2 - 4 * x)
    y_id = (z, row + 4 - 8 * y)
    diag_id = (z, 7 - row + 2 * c - 1)
    peers = [core_id, x_id, y_id, diag_id] + [(lax.rem(z + d, 4), row) for d in (1, 2, 3)]

    barrier = pltpu.get_barrier_semaphore()
    for peer in peers:
        pl.semaphore_signal(barrier, inc=1, device_id=peer, device_id_type=MESH)

    pending = []

    def send(src, dst, send_sem, recv_sem, peer):
        copy = pltpu.make_async_remote_copy(
            src_ref=src, dst_ref=dst, send_sem=send_sem, recv_sem=recv_sem,
            device_id=peer, device_id_type=MESH,
        )
        copy.start()
        pending.append(copy)
        return copy

    scales_ref[...] = scales_in[...].astype(F32)
    rows_all = design_ref.shape[0]
    owned = sketch_ref.shape[0]
    half = design_ref.shape[1] // 2

    def part(slot):
        ty = y if slot < 2 else 1 - y
        tx = x if slot % 2 == 0 else 1 - x
        base = (ty * 4 + tx * 2) * owned
        ids = lax.broadcasted_iota(jnp.int32, (owned, LANES), 0) + base
        labels = jnp.concatenate([ids + (1 - c) * owned, ids + c * owned], axis=0)
        table = jnp.concatenate(
            [
                jnp.where(labels == buckets_ref[k : k + 1, :], scales_ref[k : k + 1, :], 0.0).astype(BF16)
                for k in range(rows_all // LANES)
            ],
            axis=1,
        )
        value = jnp.dot(table, design_ref[...], preferred_element_type=F32)
        for h in range(2):
            give[slot, h] = value[:owned, h * half : (h + 1) * half]
            acc[slot, h] = value[owned:, h * half : (h + 1) * half]

    first = (x_id, y_id)
    second = (y_id, x_id)
    passed = (2, 1)
    direct = (1, 2)

    def near_send(slot, h, step):
        peer = second[h] if step == 2 else first[h]
        return send(acc.at[slot, h], near.at[h, step], near_s.at[h, step], near_r.at[h, step], peer)

    steps = {}
    from_core = {}
    order = (3, 2, 1, 0)

    def give_core(slot):
        from_core[slot] = send(give.at[slot], took.at[slot], give_s.at[slot], give_r.at[slot], core_id)

    def take_core(slot):
        from_core[slot].wait_recv()
        for h in range(2):
            acc[slot, h] = acc[slot, h] + took[slot, h]
            if slot == 3:
                steps[h, 0] = near_send(slot, h, 0)
            elif slot == direct[h]:
                steps[h, 1] = near_send(slot, h, 1)

    part(3)
    pl.semaphore_wait(barrier, len(peers))
    give_core(3)
    part(2)
    give_core(2)
    take_core(3)
    part(1)
    give_core(1)
    take_core(2)
    part(0)
    give_core(0)
    take_core(1)
    take_core(0)
    for h in range(2):
        steps[h, 0].wait_recv()
        acc[passed[h], h] = acc[passed[h], h] + near[h, 0]
        steps[h, 2] = near_send(passed[h], h, 2)
    for h in range(2):
        steps[h, 1].wait_recv()
        acc[0, h] = acc[0, h] + near[h, 1]
    for h in range(2):
        steps[h, 2].wait_recv()
        sketch_ref[:, h * half : (h + 1) * half] = acc[0, h] + near[h, 2]

    q = half // 2

    def cut(i, j):
        return sketch_ref[:, i * q : j * q]

    gsum[0:q] = tdot(cut(0, 1), cut(0, 4))
    gsum[q:half, q:] = tdot(cut(1, 2), cut(1, 4))
    gsum[q:half, 0:q] = tdot(cut(3, 4), cut(3, 4))
    value = tdot(cut(2, 3), cut(2, 4))
    gsum[half:, 0:half] = value[: q // 2]
    gsum[half:, half:] = value[q // 2 :]

    packed = gsum.shape[0]
    core_rows = packed // 2
    piece = packed // 8
    theirs = pl.ds(pl.multiple_of((1 - c) * core_rows, 8), core_rows)
    ours = pl.ds(pl.multiple_of(c * core_rows, 8), core_rows)
    send(gsum.at[theirs], gcore, gcore_s, gcore_r, core_id).wait_recv()

    def chip(slot):
        cy = y if slot < 2 else 1 - y
        cx = x if slot % 2 == 0 else 1 - x
        return pl.multiple_of((cy * 2 + cx) * piece, 8)

    plane_ids = {1: x_id, 2: y_id, 3: diag_id}
    gown[...] = gsum[ours] + gcore[...]
    copies = {
        slot: send(
            gown.at[pl.ds(chip(slot), piece)], gnear.at[slot - 1],
            gnear_s.at[slot - 1], gnear_r.at[slot - 1], plane_ids[slot],
        )
        for slot in (3, 1, 2)
    }
    total = gown[pl.ds(chip(0), piece)]
    for slot in (1, 2, 3):
        copies[slot].wait_recv()
        total = total + gnear[slot - 1]
    gz[0] = total

    def lanes_of(place):
        return pl.ds(pl.multiple_of(place * q, q), q)

    z_places = [lax.rem(z + d, 4) for d in (1, 2, 3)]
    copies = [
        send(
            gz.at[0, :, lanes_of(place)], gquart.at[d], gz_s.at[d], gz_r.at[d], (place, row)
        )
        for d, place in enumerate(z_places)
    ]
    mine = lanes_of(z)
    total = gz[0, :, mine]
    for d in range(3):
        copies[d].wait_recv()
        total = total + gquart[d]
    at = pl.ds(pl.multiple_of(c * core_rows + chip(0), 8), piece)
    gall[at, mine] = total
    for d, place in enumerate(z_places):
        ref = gall.at[at, mine]
        send(ref, ref, gz_s.at[3 + d], gz_r.at[3 + d], (place, row))
    for d in range(3):
        ref = gall.at[at, lanes_of(lax.rem(z + 3 - d, 4))]
        pltpu.make_async_remote_copy(
            src_ref=ref, dst_ref=ref, send_sem=gz_s.at[3 + d], recv_sem=gz_r.at[3 + d],
            device_id=core_id, device_id_type=MESH,
        ).wait_recv()

    def place(slot, core):
        return gall.at[pl.ds(pl.multiple_of(core * core_rows + chip(slot), 8), piece)]

    def landed(ref, sems, step):
        pltpu.make_async_remote_copy(
            src_ref=ref, dst_ref=ref, send_sem=gcore_s, recv_sem=sems.at[step],
            device_id=core_id, device_id_type=MESH,
        ).wait_recv()

    for slot in (3, 1, 2):
        send(place(0, c), place(0, c), gback_s.at[slot], gback_r.at[slot], plane_ids[slot])
    send(place(0, c), place(0, c), gpair_s.at[0], gpair_r.at[0], core_id)
    for slot in (1, 2, 3):
        landed(place(slot, c), gback_r, slot)
        send(place(slot, c), place(slot, c), gpair_s.at[slot], gpair_r.at[slot], core_id)
    for slot in range(4):
        landed(place(slot, 1 - c), gpair_r, slot)

    gram_ref[...] = gall[...]
    for copy in pending:
        copy.wait_send()


def per_device_fast(design, scales, buckets):
    row_count, col_count = design.shape
    owned = row_count // lax.axis_size("row")
    half = col_count // 2
    quarter = half // 2
    packed = quarter * 5 // 2
    grp_count = lax.axis_size("grp")
    dma = pltpu.SemaphoreType.DMA
    vmem = pl.BlockSpec(memory_space=pltpu.VMEM)
    sketch, gram = pl.pallas_call(
        embed_kernel,
        out_shape=(
            jax.ShapeDtypeStruct((owned, col_count), F32),
            jax.ShapeDtypeStruct((packed, col_count), F32),
        ),
        in_specs=[vmem, vmem, vmem],
        out_specs=(vmem, vmem),
        scratch_shapes=[
            pltpu.VMEM((row_count // LANES, LANES), F32),
            pltpu.VMEM((4, 2, owned, half), F32),
            pltpu.VMEM((4, 2, owned, half), F32),
            pltpu.VMEM((4, 2, owned, half), F32),
            pltpu.VMEM((2, 3, owned, half), F32),
            pltpu.VMEM((packed, col_count), F32),
            pltpu.VMEM((packed // 2, col_count), F32),
            pltpu.VMEM((packed // 2, col_count), F32),
            pltpu.VMEM((3, packed // 8, col_count), F32),
            pltpu.VMEM((1, packed // 8, col_count), F32),
            pltpu.VMEM((3, packed // 8, quarter), F32),
            pltpu.VMEM((packed, col_count), F32),
            dma((4,)), dma((4,)),
            dma((2, 3)), dma((2, 3)),
            dma, dma,
            dma((3,)), dma((3,)),
            dma((6,)), dma((6,)),
            dma((4,)), dma((4,)),
            dma((4,)), dma((4,)),
        ],
        compiler_params=pltpu.CompilerParams(
            collective_id=0, has_side_effects=True, vmem_limit_bytes=40 * 1024 * 1024
        ),
        name="embed",
    )(design, scales.reshape(-1, LANES), buckets.reshape(-1, LANES))
    slab, sketch = pl.pallas_call(
        functools.partial(factor_packed_kernel, 1.0 / math.sqrt(row_count * grp_count)),
        out_shape=(
            jax.ShapeDtypeStruct((col_count // grp_count, col_count), F32),
            jax.ShapeDtypeStruct((owned, col_count), F32),
        ),
        in_specs=[vmem, pl.BlockSpec(memory_space=pl.ANY)],
        out_specs=(vmem, pl.BlockSpec(memory_space=pl.ANY)),
        scratch_shapes=[pltpu.VMEM((col_count, col_count), F32), dma],
        compiler_params=pltpu.CompilerParams(vmem_limit_bytes=32 * 1024 * 1024),
        name="factor",
    )(gram, sketch)
    return (sketch, slab)


def solution(mesh):
    in_specs = (P(("grp", "row"), None), P(("grp", "row")), P(("grp", "row")))
    out_specs = (P(("grp", "row"), None), P("grp", None))
    fast = mesh.shape["grp"] == 4 and mesh.shape["row"] == 8
    return jax.shard_map(
        per_device_fast if fast else per_device_general,
        mesh=mesh, in_specs=in_specs, out_specs=out_specs, check_vma=False,
    )
```

```python
import functools
import math

import jax
import jax.numpy as jnp
from jax import lax
from jax.experimental import pallas as pl
from jax.experimental.pallas import tpu as pltpu
from jax.sharding import PartitionSpec as P

MESH = pl.DeviceIdType.MESH
F32 = jnp.float32
BF16 = jnp.bfloat16
LANES = 128
PANEL = 16


def split3(value):
    high = value.astype(BF16)
    rest = value - high.astype(F32)
    mid = rest.astype(BF16)
    low = (rest - mid.astype(F32)).astype(BF16)
    return high, mid, low


def panel_factor(panel, offset):
    size, width = panel.shape
    tiles = width // LANES
    bands = size // 8
    sub = lax.broadcasted_iota(jnp.int32, (8, LANES), 0)
    cols = {
        (b, k): jnp.broadcast_to(
            panel[8 * b : 8 * b + 8, offset + k : offset + k + 1], (8, LANES)
        )
        for k in range(size)
        for b in range(k // 8, bands)
    }
    parts = {
        (b, t): panel[8 * b : 8 * b + 8, t * LANES : (t + 1) * LANES]
        for b in range(bands)
        for t in range(tiles)
    }
    scale = [jnp.zeros((8, LANES), F32) for _ in range(bands)]
    for j in range(size):
        jb, jr = j // 8, j % 8
        inv = lax.rsqrt(cols[jb, j][jr : jr + 1, :])
        mult = {b: cols[b, j] * inv for b in range(jb, bands)}
        scale[jb] = jnp.where(sub == jr, inv, scale[jb])
        for k in range(j + 1, size):
            other = mult[k // 8][k % 8 : k % 8 + 1, :]
            for b in range(k // 8, bands):
                cols[b, k] = cols[b, k] - mult[b] * other
        pivots = [parts[jb, t][jr : jr + 1, :] * inv for t in range(tiles)]
        for b in range(jb, bands):
            if b == jb and jr == 7:
                continue
            below = jnp.where(sub > jr, mult[b], 0.0) if b == jb else mult[b]
            for t in range(tiles):
                parts[b, t] = parts[b, t] - below * pivots[t]
    return [
        jnp.concatenate([parts[b, t] * scale[b] for b in range(bands)], axis=0)
        for t in range(tiles)
    ]


def factor_block(work, base, stop, hook=None):
    for start in range(0, LANES, PANEL):
        row = base + start
        rows = panel_factor(work[row : row + PANEL, base:stop], start)
        for t, part in enumerate(rows):
            work[row : row + PANEL, base + t * LANES : base + (t + 1) * LANES] = part
        if hook is not None:
            hook()
        if start + PANEL == LANES:
            break
        splits = [split3(part) for part in rows]
        h, m, l = splits[0]
        lhs = jnp.concatenate([h, h, m, h, l, m], axis=0)
        for t, (h, m, l) in enumerate(splits):
            rhs = jnp.concatenate([h, m, h, l, h, m], axis=0)
            prod = lax.dot_general(lhs, rhs, (((0,), (0,)), ((), ())), preferred_element_type=F32)
            cs = slice(base + t * LANES, base + (t + 1) * LANES)
            work[row + PANEL : base + LANES, cs] = (
                work[row + PANEL : base + LANES, cs] - prod[start + PANEL :, :]
            )


def tdot(left, right):
    return lax.dot_general(
        left, right, (((0,), (0,)), ((), ())),
        precision=lax.Precision.HIGHEST, preferred_element_type=F32,
    )


def trail(work, base, last, stop):
    for left in range(base + LANES, last, LANES):
        work[left : left + LANES, left:stop] = work[left : left + LANES, left:stop] - tdot(
            work[base : base + LANES, left : left + LANES], work[base : base + LANES, left:stop]
        )


def write_rows(grp, scale, out_ref, work):
    size = work.shape[0]
    count = out_ref.shape[0]
    first = pl.multiple_of(grp * count, count)
    rows = first + lax.broadcasted_iota(jnp.int32, (count, size), 0)
    cols = lax.broadcasted_iota(jnp.int32, (count, size), 1)
    value = work[pl.ds(first, count), :] * scale
    out_ref[...] = jnp.where(cols >= rows, value, 0.0)


def factor_kernel(scale, gram_ref, out_ref, work):
    size = work.shape[0]
    work[...] = gram_ref[...]
    for base in range(0, size, LANES):
        factor_block(work, base, size)
        trail(work, base, size, size)
    write_rows(lax.axis_index("grp"), scale, out_ref, work)


def factor_packed_kernel(scale, gram_ref, sketch_ref, out_ref, sketch_out, work, copy_sem):
    copy = pltpu.make_async_copy(sketch_ref, sketch_out, copy_sem)
    copy.start()
    size = work.shape[0]
    half = size // 2
    q = half // 2
    work[0:q] = gram_ref[0:q]
    work[q:half, q:] = gram_ref[q:half, q:]
    work[3 * q :, 3 * q :] = gram_ref[q:half, 0:q]
    work[half : half + q // 2, half:] = gram_ref[half:, 0:half]
    work[half + q // 2 : 3 * q, half:] = gram_ref[half:, half:]
    for base in range(0, size, LANES):
        factor_block(work, base, size)
        trail(work, base, size, size)
    write_rows(lax.axis_index("grp"), scale, out_ref, work)
    copy.wait()


def factor_call(gram, slab_rows, scale):
    size = gram.shape[0]
    vmem = pl.BlockSpec(memory_space=pltpu.VMEM)
    return pl.pallas_call(
        functools.partial(factor_kernel, scale),
        out_shape=jax.ShapeDtypeStruct((slab_rows, size), F32),
        in_specs=[vmem],
        out_specs=vmem,
        scratch_shapes=[pltpu.VMEM((size, size), F32)],
        compiler_params=pltpu.CompilerParams(vmem_limit_bytes=32 * 1024 * 1024),
        name="factor",
    )(gram)


def self_gram(matrix):
    return lax.dot_general(
        matrix,
        matrix,
        (((0,), (0,)), ((), ())),
        precision=lax.Precision.HIGHEST,
        preferred_element_type=F32,
    )


def per_device_general(design, scales, buckets):
    row_count = design.shape[0]
    col_count = design.shape[1]
    row_parts = lax.axis_size("row")
    owned_rows = row_count // row_parts
    label_ids = lax.iota(jnp.int32, row_count)
    onehot_table = jnp.where(
        label_ids[:, None] == buckets[None, :], scales[None, :], jnp.zeros((), BF16)
    )
    partial_value = jnp.dot(onehot_table, design, preferred_element_type=F32).reshape(
        row_parts, owned_rows, col_count
    )
    arrived = lax.all_to_all(partial_value, "row", split_axis=0, concat_axis=0, tiled=True)
    sketch = jnp.sum(arrived, axis=0)
    whole_gram = lax.psum(self_gram(sketch), ("grp", "row"))
    grp_count = lax.axis_size("grp")
    scale = 1.0 / math.sqrt(row_count * grp_count)
    slab = factor_call(whole_gram, col_count // grp_count, scale)
    return (sketch, slab)


def embed_kernel(
    design_hbm, scales_in, buckets_ref, sketch_ref, gram_ref,
    design_ref, load_s, scales_ref,
    give, took, acc, near, gsum, gcore, gown, gnear, gz, gquart, gall,
    give_s, give_r, near_s, near_r, gcore_s, gcore_r, gnear_s, gnear_r, gz_s, gz_r,
    gback_s, gback_r, gpair_s, gpair_r,
):
    z = lax.axis_index("grp")
    row = lax.axis_index("row")
    c = lax.rem(row, 2)
    x = lax.rem(row // 2, 2)
    y = row // 4
    core_id = (z, row + 1 - 2 * c)
    x_id = (z, row + 2 - 4 * x)
    y_id = (z, row + 4 - 8 * y)
    diag_id = (z, 7 - row + 2 * c - 1)
    peers = [core_id, x_id, y_id, diag_id] + [(lax.rem(z + d, 4), row) for d in (1, 2, 3)]

    load = pltpu.make_async_copy(design_hbm, design_ref, load_s)
    load.start()
    barrier = pltpu.get_barrier_semaphore()
    for peer in peers:
        pl.semaphore_signal(barrier, inc=1, device_id=peer, device_id_type=MESH)

    pending = []

    def send(src, dst, send_sem, recv_sem, peer):
        copy = pltpu.make_async_remote_copy(
            src_ref=src, dst_ref=dst, send_sem=send_sem, recv_sem=recv_sem,
            device_id=peer, device_id_type=MESH,
        )
        copy.start()
        pending.append(copy)
        return copy

    scales_ref[...] = scales_in[...].astype(F32)
    rows_all = design_ref.shape[0]
    owned = sketch_ref.shape[0]
    half = design_ref.shape[1] // 2

    def part(slot):
        ty = y if slot < 2 else 1 - y
        tx = x if slot % 2 == 0 else 1 - x
        base = (ty * 4 + tx * 2) * owned
        ids = lax.broadcasted_iota(jnp.int32, (owned, LANES), 0) + base
        labels = jnp.concatenate([ids + (1 - c) * owned, ids + c * owned], axis=0)
        table = jnp.concatenate(
            [
                jnp.where(labels == buckets_ref[k : k + 1, :], scales_ref[k : k + 1, :], 0.0).astype(BF16)
                for k in range(rows_all // LANES)
            ],
            axis=1,
        )
        if slot == 3:
            load.wait()
        value = jnp.dot(table, design_ref[...], preferred_element_type=F32)
        for h in range(2):
            give[slot, h] = value[:owned, h * half : (h + 1) * half]
            acc[slot, h] = value[owned:, h * half : (h + 1) * half]

    first = (x_id, y_id)
    second = (y_id, x_id)
    passed = (2, 1)
    direct = (1, 2)

    def near_send(slot, h, step):
        peer = second[h] if step == 2 else first[h]
        return send(acc.at[slot, h], near.at[h, step], near_s.at[h, step], near_r.at[h, step], peer)

    steps = {}
    from_core = {}
    order = (3, 2, 1, 0)

    def give_core(slot):
        from_core[slot] = send(give.at[slot], took.at[slot], give_s.at[slot], give_r.at[slot], core_id)

    def take_core(slot):
        from_core[slot].wait_recv()
        for h in range(2):
            acc[slot, h] = acc[slot, h] + took[slot, h]
            if slot == 3:
                steps[h, 0] = near_send(slot, h, 0)
            elif slot == direct[h]:
                steps[h, 1] = near_send(slot, h, 1)

    part(3)
    pl.semaphore_wait(barrier, len(peers))
    give_core(3)
    part(2)
    give_core(2)
    take_core(3)
    part(1)
    give_core(1)
    take_core(2)
    part(0)
    give_core(0)
    take_core(1)
    take_core(0)
    for h in range(2):
        steps[h, 0].wait_recv()
        acc[passed[h], h] = acc[passed[h], h] + near[h, 0]
        steps[h, 2] = near_send(passed[h], h, 2)
    for h in range(2):
        steps[h, 1].wait_recv()
        acc[0, h] = acc[0, h] + near[h, 1]
    for h in range(2):
        steps[h, 2].wait_recv()
        sketch_ref[:, h * half : (h + 1) * half] = acc[0, h] + near[h, 2]

    q = half // 2

    def cut(i, j):
        return sketch_ref[:, i * q : j * q]

    gsum[0:q] = tdot(cut(0, 1), cut(0, 4))
    gsum[q:half, q:] = tdot(cut(1, 2), cut(1, 4))
    gsum[q:half, 0:q] = tdot(cut(3, 4), cut(3, 4))
    value = tdot(cut(2, 3), cut(2, 4))
    gsum[half:, 0:half] = value[: q // 2]
    gsum[half:, half:] = value[q // 2 :]

    packed = gsum.shape[0]
    core_rows = packed // 2
    piece = packed // 8
    theirs = pl.ds(pl.multiple_of((1 - c) * core_rows, 8), core_rows)
    ours = pl.ds(pl.multiple_of(c * core_rows, 8), core_rows)
    send(gsum.at[theirs], gcore, gcore_s, gcore_r, core_id).wait_recv()

    def chip(slot):
        cy = y if slot < 2 else 1 - y
        cx = x if slot % 2 == 0 else 1 - x
        return pl.multiple_of((cy * 2 + cx) * piece, 8)

    plane_ids = {1: x_id, 2: y_id, 3: diag_id}
    gown[...] = gsum[ours] + gcore[...]
    copies = {
        slot: send(
            gown.at[pl.ds(chip(slot), piece)], gnear.at[slot - 1],
            gnear_s.at[slot - 1], gnear_r.at[slot - 1], plane_ids[slot],
        )
        for slot in (3, 1, 2)
    }
    total = gown[pl.ds(chip(0), piece)]
    for slot in (1, 2, 3):
        copies[slot].wait_recv()
        total = total + gnear[slot - 1]
    gz[0] = total

    def lanes_of(place):
        return pl.ds(pl.multiple_of(place * q, q), q)

    z_places = [lax.rem(z + d, 4) for d in (1, 2, 3)]
    copies = [
        send(
            gz.at[0, :, lanes_of(place)], gquart.at[d], gz_s.at[d], gz_r.at[d], (place, row)
        )
        for d, place in enumerate(z_places)
    ]
    mine = lanes_of(z)
    total = gz[0, :, mine]
    for d in range(3):
        copies[d].wait_recv()
        total = total + gquart[d]
    at = pl.ds(pl.multiple_of(c * core_rows + chip(0), 8), piece)
    gall[at, mine] = total
    for d, place in enumerate(z_places):
        ref = gall.at[at, mine]
        send(ref, ref, gz_s.at[3 + d], gz_r.at[3 + d], (place, row))
    for d in range(3):
        ref = gall.at[at, lanes_of(lax.rem(z + 3 - d, 4))]
        pltpu.make_async_remote_copy(
            src_ref=ref, dst_ref=ref, send_sem=gz_s.at[3 + d], recv_sem=gz_r.at[3 + d],
            device_id=core_id, device_id_type=MESH,
        ).wait_recv()

    def place(slot, core):
        return gall.at[pl.ds(pl.multiple_of(core * core_rows + chip(slot), 8), piece)]

    def landed(ref, sems, step):
        pltpu.make_async_remote_copy(
            src_ref=ref, dst_ref=ref, send_sem=gcore_s, recv_sem=sems.at[step],
            device_id=core_id, device_id_type=MESH,
        ).wait_recv()

    for slot in (3, 1, 2):
        send(place(0, c), place(0, c), gback_s.at[slot], gback_r.at[slot], plane_ids[slot])
    send(place(0, c), place(0, c), gpair_s.at[0], gpair_r.at[0], core_id)
    for slot in (1, 2, 3):
        landed(place(slot, c), gback_r, slot)
        send(place(slot, c), place(slot, c), gpair_s.at[slot], gpair_r.at[slot], core_id)
    for slot in range(4):
        landed(place(slot, 1 - c), gpair_r, slot)

    gram_ref[...] = gall[...]
    for copy in pending:
        copy.wait_send()


def per_device_fast(design, scales, buckets):
    row_count, col_count = design.shape
    owned = row_count // lax.axis_size("row")
    half = col_count // 2
    quarter = half // 2
    packed = quarter * 5 // 2
    grp_count = lax.axis_size("grp")
    dma = pltpu.SemaphoreType.DMA
    vmem = pl.BlockSpec(memory_space=pltpu.VMEM)
    sketch, gram = pl.pallas_call(
        embed_kernel,
        out_shape=(
            jax.ShapeDtypeStruct((owned, col_count), F32),
            jax.ShapeDtypeStruct((packed, col_count), F32),
        ),
        in_specs=[pl.BlockSpec(memory_space=pl.ANY), vmem, vmem],
        out_specs=(vmem, vmem),
        scratch_shapes=[
            pltpu.VMEM((row_count, col_count), BF16),
            dma,
            pltpu.VMEM((row_count // LANES, LANES), F32),
            pltpu.VMEM((4, 2, owned, half), F32),
            pltpu.VMEM((4, 2, owned, half), F32),
            pltpu.VMEM((4, 2, owned, half), F32),
            pltpu.VMEM((2, 3, owned, half), F32),
            pltpu.VMEM((packed, col_count), F32),
            pltpu.VMEM((packed // 2, col_count), F32),
            pltpu.VMEM((packed // 2, col_count), F32),
            pltpu.VMEM((3, packed // 8, col_count), F32),
            pltpu.VMEM((1, packed // 8, col_count), F32),
            pltpu.VMEM((3, packed // 8, quarter), F32),
            pltpu.VMEM((packed, col_count), F32),
            dma((4,)), dma((4,)),
            dma((2, 3)), dma((2, 3)),
            dma, dma,
            dma((3,)), dma((3,)),
            dma((6,)), dma((6,)),
            dma((4,)), dma((4,)),
            dma((4,)), dma((4,)),
        ],
        compiler_params=pltpu.CompilerParams(
            collective_id=0, has_side_effects=True, vmem_limit_bytes=52 * 1024 * 1024
        ),
        name="embed",
    )(design, scales.reshape(-1, LANES), buckets.reshape(-1, LANES))
    slab, sketch = pl.pallas_call(
        functools.partial(factor_packed_kernel, 1.0 / math.sqrt(row_count * grp_count)),
        out_shape=(
            jax.ShapeDtypeStruct((col_count // grp_count, col_count), F32),
            jax.ShapeDtypeStruct((owned, col_count), F32),
        ),
        in_specs=[vmem, pl.BlockSpec(memory_space=pl.ANY)],
        out_specs=(vmem, pl.BlockSpec(memory_space=pl.ANY)),
        scratch_shapes=[pltpu.VMEM((col_count, col_count), F32), dma],
        compiler_params=pltpu.CompilerParams(vmem_limit_bytes=32 * 1024 * 1024),
        name="factor",
    )(gram, sketch)
    return (sketch, slab)


def solution(mesh):
    in_specs = (P(("grp", "row"), None), P(("grp", "row")), P(("grp", "row")))
    out_specs = (P(("grp", "row"), None), P("grp", None))
    fast = mesh.shape["grp"] == 4 and mesh.shape["row"] == 8
    return jax.shard_map(
        per_device_fast if fast else per_device_general,
        mesh=mesh, in_specs=in_specs, out_specs=out_specs, check_vma=False,
    )
```

```python
import functools
import math

import jax
import jax.numpy as jnp
from jax import lax
from jax.experimental import pallas as pl
from jax.experimental.pallas import tpu as pltpu
from jax.sharding import PartitionSpec as P

MESH = pl.DeviceIdType.MESH
F32 = jnp.float32
BF16 = jnp.bfloat16
LANES = 128
PANEL = 32


def split3(value):
    high = value.astype(BF16)
    rest = value - high.astype(F32)
    mid = rest.astype(BF16)
    low = (rest - mid.astype(F32)).astype(BF16)
    return high, mid, low


def panel_factor(panel, offset):
    size, width = panel.shape
    tiles = width // LANES
    bands = size // 8
    sub = lax.broadcasted_iota(jnp.int32, (8, LANES), 0)
    cols = {
        (b, k): jnp.broadcast_to(
            panel[8 * b : 8 * b + 8, offset + k : offset + k + 1], (8, LANES)
        )
        for k in range(size)
        for b in range(k // 8, bands)
    }
    parts = {
        (b, t): panel[8 * b : 8 * b + 8, t * LANES : (t + 1) * LANES]
        for b in range(bands)
        for t in range(tiles)
    }
    scale = [jnp.zeros((8, LANES), F32) for _ in range(bands)]
    for j in range(size):
        jb, jr = j // 8, j % 8
        inv = lax.rsqrt(cols[jb, j][jr : jr + 1, :])
        mult = {b: cols[b, j] * inv for b in range(jb, bands)}
        scale[jb] = jnp.where(sub == jr, inv, scale[jb])
        for k in range(j + 1, size):
            other = mult[k // 8][k % 8 : k % 8 + 1, :]
            for b in range(k // 8, bands):
                cols[b, k] = cols[b, k] - mult[b] * other
        pivots = [parts[jb, t][jr : jr + 1, :] * inv for t in range(tiles)]
        for b in range(jb, bands):
            if b == jb and jr == 7:
                continue
            below = jnp.where(sub > jr, mult[b], 0.0) if b == jb else mult[b]
            for t in range(tiles):
                parts[b, t] = parts[b, t] - below * pivots[t]
    return [
        jnp.concatenate([parts[b, t] * scale[b] for b in range(bands)], axis=0)
        for t in range(tiles)
    ]


def factor_block(work, base, stop, hook=None):
    for start in range(0, LANES, PANEL):
        row = base + start
        rows = panel_factor(work[row : row + PANEL, base:stop], start)
        for t, part in enumerate(rows):
            work[row : row + PANEL, base + t * LANES : base + (t + 1) * LANES] = part
        if hook is not None:
            hook()
        if start + PANEL == LANES:
            break
        splits = [split3(part) for part in rows]
        h, m, l = splits[0]
        lhs = jnp.concatenate([h, h, m, h, l, m], axis=0)
        for t, (h, m, l) in enumerate(splits):
            rhs = jnp.concatenate([h, m, h, l, h, m], axis=0)
            prod = lax.dot_general(lhs, rhs, (((0,), (0,)), ((), ())), preferred_element_type=F32)
            cs = slice(base + t * LANES, base + (t + 1) * LANES)
            work[row + PANEL : base + LANES, cs] = (
                work[row + PANEL : base + LANES, cs] - prod[start + PANEL :, :]
            )


def tdot(left, right):
    return lax.dot_general(
        left, right, (((0,), (0,)), ((), ())),
        precision=lax.Precision.HIGHEST, preferred_element_type=F32,
    )


def trail(work, base, last, stop):
    for left in range(base + LANES, last, LANES):
        work[left : left + LANES, left:stop] = work[left : left + LANES, left:stop] - tdot(
            work[base : base + LANES, left : left + LANES], work[base : base + LANES, left:stop]
        )


def write_rows(grp, scale, out_ref, work):
    size = work.shape[0]
    count = out_ref.shape[0]
    first = pl.multiple_of(grp * count, count)
    rows = first + lax.broadcasted_iota(jnp.int32, (count, size), 0)
    cols = lax.broadcasted_iota(jnp.int32, (count, size), 1)
    value = work[pl.ds(first, count), :] * scale
    out_ref[...] = jnp.where(cols >= rows, value, 0.0)


def factor_kernel(scale, gram_ref, out_ref, work):
    size = work.shape[0]
    work[...] = gram_ref[...]
    for base in range(0, size, LANES):
        factor_block(work, base, size)
        trail(work, base, size, size)
    write_rows(lax.axis_index("grp"), scale, out_ref, work)


def factor_packed_kernel(scale, gram_ref, sketch_ref, out_ref, sketch_out, work, copy_sem):
    copy = pltpu.make_async_copy(sketch_ref, sketch_out, copy_sem)
    copy.start()
    size = work.shape[0]
    half = size // 2
    q = half // 2
    work[0:q] = gram_ref[0:q]
    work[q:half, q:] = gram_ref[q:half, q:]
    work[3 * q :, 3 * q :] = gram_ref[q:half, 0:q]
    work[half : half + q // 2, half:] = gram_ref[half:, 0:half]
    work[half + q // 2 : 3 * q, half:] = gram_ref[half:, half:]
    for base in range(0, size, LANES):
        factor_block(work, base, size)
        trail(work, base, size, size)
    write_rows(lax.axis_index("grp"), scale, out_ref, work)
    copy.wait()


def factor_call(gram, slab_rows, scale):
    size = gram.shape[0]
    vmem = pl.BlockSpec(memory_space=pltpu.VMEM)
    return pl.pallas_call(
        functools.partial(factor_kernel, scale),
        out_shape=jax.ShapeDtypeStruct((slab_rows, size), F32),
        in_specs=[vmem],
        out_specs=vmem,
        scratch_shapes=[pltpu.VMEM((size, size), F32)],
        compiler_params=pltpu.CompilerParams(vmem_limit_bytes=32 * 1024 * 1024),
        name="factor",
    )(gram)


def self_gram(matrix):
    return lax.dot_general(
        matrix,
        matrix,
        (((0,), (0,)), ((), ())),
        precision=lax.Precision.HIGHEST,
        preferred_element_type=F32,
    )


def per_device_general(design, scales, buckets):
    row_count = design.shape[0]
    col_count = design.shape[1]
    row_parts = lax.axis_size("row")
    owned_rows = row_count // row_parts
    label_ids = lax.iota(jnp.int32, row_count)
    onehot_table = jnp.where(
        label_ids[:, None] == buckets[None, :], scales[None, :], jnp.zeros((), BF16)
    )
    partial_value = jnp.dot(onehot_table, design, preferred_element_type=F32).reshape(
        row_parts, owned_rows, col_count
    )
    arrived = lax.all_to_all(partial_value, "row", split_axis=0, concat_axis=0, tiled=True)
    sketch = jnp.sum(arrived, axis=0)
    whole_gram = lax.psum(self_gram(sketch), ("grp", "row"))
    grp_count = lax.axis_size("grp")
    scale = 1.0 / math.sqrt(row_count * grp_count)
    slab = factor_call(whole_gram, col_count // grp_count, scale)
    return (sketch, slab)


def embed_kernel(
    design_hbm, scales_in, buckets_ref, sketch_ref, gram_ref,
    design_ref, load_s, scales_ref,
    give, took, acc, near, gsum, gcore, gown, gnear, gz, gquart, gall,
    give_s, give_r, near_s, near_r, gcore_s, gcore_r, gnear_s, gnear_r, gz_s, gz_r,
    gback_s, gback_r, gpair_s, gpair_r,
):
    z = lax.axis_index("grp")
    row = lax.axis_index("row")
    c = lax.rem(row, 2)
    x = lax.rem(row // 2, 2)
    y = row // 4
    core_id = (z, row + 1 - 2 * c)
    x_id = (z, row + 2 - 4 * x)
    y_id = (z, row + 4 - 8 * y)
    diag_id = (z, 7 - row + 2 * c - 1)
    peers = [core_id, x_id, y_id, diag_id] + [(lax.rem(z + d, 4), row) for d in (1, 2, 3)]

    load = pltpu.make_async_copy(design_hbm, design_ref, load_s)
    load.start()
    barrier = pltpu.get_barrier_semaphore()
    for peer in peers:
        pl.semaphore_signal(barrier, inc=1, device_id=peer, device_id_type=MESH)

    pending = []

    def send(src, dst, send_sem, recv_sem, peer):
        copy = pltpu.make_async_remote_copy(
            src_ref=src, dst_ref=dst, send_sem=send_sem, recv_sem=recv_sem,
            device_id=peer, device_id_type=MESH,
        )
        copy.start()
        pending.append(copy)
        return copy

    scales_ref[...] = scales_in[...].astype(F32)
    rows_all = design_ref.shape[0]
    owned = sketch_ref.shape[0]
    half = design_ref.shape[1] // 2

    def part(slot):
        ty = y if slot < 2 else 1 - y
        tx = x if slot % 2 == 0 else 1 - x
        base = (ty * 4 + tx * 2) * owned
        ids = lax.broadcasted_iota(jnp.int32, (owned, LANES), 0) + base
        labels = jnp.concatenate([ids + (1 - c) * owned, ids + c * owned], axis=0)
        table = jnp.concatenate(
            [
                jnp.where(labels == buckets_ref[k : k + 1, :], scales_ref[k : k + 1, :], 0.0).astype(BF16)
                for k in range(rows_all // LANES)
            ],
            axis=1,
        )
        if slot == 3:
            load.wait()
        value = jnp.dot(table, design_ref[...], preferred_element_type=F32)
        for h in range(2):
            give[slot, h] = value[:owned, h * half : (h + 1) * half]
            acc[slot, h] = value[owned:, h * half : (h + 1) * half]

    first = (x_id, y_id)
    second = (y_id, x_id)
    passed = (2, 1)
    direct = (1, 2)

    def near_send(slot, h, step):
        peer = second[h] if step == 2 else first[h]
        return send(acc.at[slot, h], near.at[h, step], near_s.at[h, step], near_r.at[h, step], peer)

    steps = {}
    from_core = {}
    order = (3, 2, 1, 0)

    def give_core(slot):
        from_core[slot] = send(give.at[slot], took.at[slot], give_s.at[slot], give_r.at[slot], core_id)

    def take_core(slot):
        from_core[slot].wait_recv()
        for h in range(2):
            acc[slot, h] = acc[slot, h] + took[slot, h]
            if slot == 3:
                steps[h, 0] = near_send(slot, h, 0)
            elif slot == direct[h]:
                steps[h, 1] = near_send(slot, h, 1)

    part(3)
    pl.semaphore_wait(barrier, len(peers))
    give_core(3)
    part(2)
    give_core(2)
    take_core(3)
    part(1)
    give_core(1)
    take_core(2)
    part(0)
    give_core(0)
    take_core(1)
    take_core(0)
    for h in range(2):
        steps[h, 0].wait_recv()
        acc[passed[h], h] = acc[passed[h], h] + near[h, 0]
        steps[h, 2] = near_send(passed[h], h, 2)
    for h in range(2):
        steps[h, 1].wait_recv()
        acc[0, h] = acc[0, h] + near[h, 1]
    for h in range(2):
        steps[h, 2].wait_recv()
        sketch_ref[:, h * half : (h + 1) * half] = acc[0, h] + near[h, 2]

    q = half // 2

    def cut(i, j):
        return sketch_ref[:, i * q : j * q]

    gsum[0:q] = tdot(cut(0, 1), cut(0, 4))
    gsum[q:half, q:] = tdot(cut(1, 2), cut(1, 4))
    gsum[q:half, 0:q] = tdot(cut(3, 4), cut(3, 4))
    value = tdot(cut(2, 3), cut(2, 4))
    gsum[half:, 0:half] = value[: q // 2]
    gsum[half:, half:] = value[q // 2 :]

    packed = gsum.shape[0]
    core_rows = packed // 2
    piece = packed // 8
    theirs = pl.ds(pl.multiple_of((1 - c) * core_rows, 8), core_rows)
    ours = pl.ds(pl.multiple_of(c * core_rows, 8), core_rows)
    send(gsum.at[theirs], gcore, gcore_s, gcore_r, core_id).wait_recv()

    def chip(slot):
        cy = y if slot < 2 else 1 - y
        cx = x if slot % 2 == 0 else 1 - x
        return pl.multiple_of((cy * 2 + cx) * piece, 8)

    plane_ids = {1: x_id, 2: y_id, 3: diag_id}
    gown[...] = gsum[ours] + gcore[...]
    copies = {
        slot: send(
            gown.at[pl.ds(chip(slot), piece)], gnear.at[slot - 1],
            gnear_s.at[slot - 1], gnear_r.at[slot - 1], plane_ids[slot],
        )
        for slot in (3, 1, 2)
    }
    total = gown[pl.ds(chip(0), piece)]
    for slot in (1, 2, 3):
        copies[slot].wait_recv()
        total = total + gnear[slot - 1]
    gz[0] = total

    def lanes_of(place):
        return pl.ds(pl.multiple_of(place * q, q), q)

    z_places = [lax.rem(z + d, 4) for d in (1, 2, 3)]
    copies = [
        send(
            gz.at[0, :, lanes_of(place)], gquart.at[d], gz_s.at[d], gz_r.at[d], (place, row)
        )
        for d, place in enumerate(z_places)
    ]
    mine = lanes_of(z)
    total = gz[0, :, mine]
    for d in range(3):
        copies[d].wait_recv()
        total = total + gquart[d]
    at = pl.ds(pl.multiple_of(c * core_rows + chip(0), 8), piece)
    gall[at, mine] = total
    for d, place in enumerate(z_places):
        ref = gall.at[at, mine]
        send(ref, ref, gz_s.at[3 + d], gz_r.at[3 + d], (place, row))
    for d in range(3):
        ref = gall.at[at, lanes_of(lax.rem(z + 3 - d, 4))]
        pltpu.make_async_remote_copy(
            src_ref=ref, dst_ref=ref, send_sem=gz_s.at[3 + d], recv_sem=gz_r.at[3 + d],
            device_id=core_id, device_id_type=MESH,
        ).wait_recv()

    def place(slot, core):
        return gall.at[pl.ds(pl.multiple_of(core * core_rows + chip(slot), 8), piece)]

    def landed(ref, sems, step):
        pltpu.make_async_remote_copy(
            src_ref=ref, dst_ref=ref, send_sem=gcore_s, recv_sem=sems.at[step],
            device_id=core_id, device_id_type=MESH,
        ).wait_recv()

    for slot in (3, 1, 2):
        send(place(0, c), place(0, c), gback_s.at[slot], gback_r.at[slot], plane_ids[slot])
    send(place(0, c), place(0, c), gpair_s.at[0], gpair_r.at[0], core_id)
    for slot in (1, 2, 3):
        landed(place(slot, c), gback_r, slot)
        send(place(slot, c), place(slot, c), gpair_s.at[slot], gpair_r.at[slot], core_id)
    for slot in range(4):
        landed(place(slot, 1 - c), gpair_r, slot)

    gram_ref[...] = gall[...]
    for copy in pending:
        copy.wait_send()


def per_device_fast(design, scales, buckets):
    row_count, col_count = design.shape
    owned = row_count // lax.axis_size("row")
    half = col_count // 2
    quarter = half // 2
    packed = quarter * 5 // 2
    grp_count = lax.axis_size("grp")
    dma = pltpu.SemaphoreType.DMA
    vmem = pl.BlockSpec(memory_space=pltpu.VMEM)
    sketch, gram = pl.pallas_call(
        embed_kernel,
        out_shape=(
            jax.ShapeDtypeStruct((owned, col_count), F32),
            jax.ShapeDtypeStruct((packed, col_count), F32),
        ),
        in_specs=[pl.BlockSpec(memory_space=pl.ANY), vmem, vmem],
        out_specs=(vmem, vmem),
        scratch_shapes=[
            pltpu.VMEM((row_count, col_count), BF16),
            dma,
            pltpu.VMEM((row_count // LANES, LANES), F32),
            pltpu.VMEM((4, 2, owned, half), F32),
            pltpu.VMEM((4, 2, owned, half), F32),
            pltpu.VMEM((4, 2, owned, half), F32),
            pltpu.VMEM((2, 3, owned, half), F32),
            pltpu.VMEM((packed, col_count), F32),
            pltpu.VMEM((packed // 2, col_count), F32),
            pltpu.VMEM((packed // 2, col_count), F32),
            pltpu.VMEM((3, packed // 8, col_count), F32),
            pltpu.VMEM((1, packed // 8, col_count), F32),
            pltpu.VMEM((3, packed // 8, quarter), F32),
            pltpu.VMEM((packed, col_count), F32),
            dma((4,)), dma((4,)),
            dma((2, 3)), dma((2, 3)),
            dma, dma,
            dma((3,)), dma((3,)),
            dma((6,)), dma((6,)),
            dma((4,)), dma((4,)),
            dma((4,)), dma((4,)),
        ],
        compiler_params=pltpu.CompilerParams(
            collective_id=0, has_side_effects=True, vmem_limit_bytes=52 * 1024 * 1024
        ),
        name="embed",
    )(design, scales.reshape(-1, LANES), buckets.reshape(-1, LANES))
    slab, sketch = pl.pallas_call(
        functools.partial(factor_packed_kernel, 1.0 / math.sqrt(row_count * grp_count)),
        out_shape=(
            jax.ShapeDtypeStruct((col_count // grp_count, col_count), F32),
            jax.ShapeDtypeStruct((owned, col_count), F32),
        ),
        in_specs=[vmem, pl.BlockSpec(memory_space=pl.ANY)],
        out_specs=(vmem, pl.BlockSpec(memory_space=pl.ANY)),
        scratch_shapes=[pltpu.VMEM((col_count, col_count), F32), dma],
        compiler_params=pltpu.CompilerParams(vmem_limit_bytes=32 * 1024 * 1024),
        name="factor",
    )(gram, sketch)
    return (sketch, slab)


def solution(mesh):
    in_specs = (P(("grp", "row"), None), P(("grp", "row")), P(("grp", "row")))
    out_specs = (P(("grp", "row"), None), P("grp", None))
    fast = mesh.shape["grp"] == 4 and mesh.shape["row"] == 8
    return jax.shard_map(
        per_device_fast if fast else per_device_general,
        mesh=mesh, in_specs=in_specs, out_specs=out_specs, check_vma=False,
    )
```
